512 devices in a mesh: row: 64 (over x, z, core), col: 8 (over y).
Axes of the slice: x: 4, y: 8, z: 8, core: 2. Of those that a mesh axis runs over, the one named last changes fastest.
Arguments:
- src_points: bfloat16 [262144, 64], P('row'), may hold values from -36 to 36
- tgt_points: bfloat16 [65536, 64], P('col'), may hold values from -36 to 36
- src_counts: int32 [1024], P('row'), may hold values from 64 to 256, as said below
- tgt_counts: int32 [256], P('col'), may hold values from 64 to 256, as said below
- tile_list: int32 [64, 8, 48, 2], P('row', 'col'), may hold values from 0 to 31, as said below
- tile_count: int32 [64, 8], P('row', 'col'), may hold values from 16 to 48, as said below
Outputs:
- src_potential: float32 [262144], P('row')
- tgt_potential: float32 [65536], P('col')
The draws below stay inside these ranges and needn't reach their ends.
Inputs may be any that keep to these rules, and one draw needn't show every extreme that they name: The first src_counts[b] slots of source block b are real; some block is full. The first tgt_counts[b] slots of target block b are real; some block is full. `tile_list`: entries (k, l) with k < 16 and l < 32; the pairs of one device differ; slot k < 16 of every device holds source block k; every target block is in a live slot of some device. `tile_count`: some device has all 48 slots live.
All inputs are finite; a program needn't handle non-finite values.
Results may differ from the reference program's by a relative error of at most 0.0003.
Values sent between devices are 32-bit elements; how exact they have to be, the bound alone decides.
No kernel may reach another device: no remote copies, remote signals or barrier semaphores. Data moves between devices by JAX's collectives and lax.ppermute only.
A program may use at most 64 MiB of HBM per device.

```python
import jax
import jax.numpy as jnp
from jax import lax

DIM = 64
BLOCK = 256
SB_DEV = 16
TB_DEV = 32
ITERS = 3
TILES_DEV = 48
ROW_GROUPS = 64
COL_GROUPS = 8
NS = 262144
NT = 65536


def rising_counts(key, nblocks):
    steps = jnp.arange(nblocks, dtype=jnp.int32)
    base = BLOCK // 4 + 3 * BLOCK // 4 * steps // nblocks
    noise = jax.random.randint(key, (nblocks,), 0, BLOCK // 4 + 1)
    counts = jnp.minimum(base + noise, BLOCK)
    return jnp.where(steps == nblocks - 1, BLOCK, counts).astype(jnp.int32)


def draw_src_points(key, part):
    key = jax.random.fold_in(key, 21)
    values = jnp.clip(jax.random.normal(key, (NS, DIM), jnp.float32), -6.0, 6.0)
    return values.astype(jnp.bfloat16)


def draw_tgt_points(key, part):
    key = jax.random.fold_in(key, 22)
    values = jnp.clip(jax.random.normal(key, (NT, DIM), jnp.float32), -6.0, 6.0)
    return values.astype(jnp.bfloat16)


def draw_src_counts(key, part):
    key = jax.random.fold_in(key, 5)
    return rising_counts(key, ROW_GROUPS * SB_DEV)


def draw_tgt_counts(key, part):
    key = jax.random.fold_in(key, 6)
    return rising_counts(key, COL_GROUPS * TB_DEV)


def draw_tile_list(key, part):
    key = jax.random.fold_in(key, 11)
    devices = ROW_GROUPS * COL_GROUPS
    keys = jax.random.split(key, devices)

    def one_device(subkey, index):
        rowdev = index // COL_GROUPS
        every = jnp.arange(SB_DEV * TB_DEV, dtype=jnp.int32)
        rowblk = every // TB_DEV
        colblk = every % TB_DEV
        basic = colblk == (rowblk + rowdev * SB_DEV) % TB_DEV
        ranks = jax.random.permutation(subkey, SB_DEV * TB_DEV).astype(jnp.int32)
        scores = jnp.where(basic, rowblk, SB_DEV + ranks)
        order = jnp.argsort(scores, stable=True)[:TILES_DEV]
        return jnp.stack([rowblk[order], colblk[order]], axis=-1)
    result = jax.vmap(one_device)(keys, jnp.arange(devices, dtype=jnp.int32))
    return result.reshape(ROW_GROUPS, COL_GROUPS, TILES_DEV, 2).astype(jnp.int32)


def draw_tile_count(key, part):
    key = jax.random.fold_in(key, 12)
    first, second = jax.random.split(key)
    devices = ROW_GROUPS * COL_GROUPS
    spread = TILES_DEV - SB_DEV
    draws = jax.random.randint(first, (devices,), 0, spread + 1)
    extra = draws * draws * draws // (spread * spread)
    fullest = jax.random.randint(second, (), 0, devices)
    counts = jnp.where(jnp.arange(devices) == fullest, TILES_DEV, SB_DEV + extra)
    return counts.reshape(ROW_GROUPS, COL_GROUPS).astype(jnp.int32)


def setup_inputs(seed: int = 0) -> dict:
    key_list = jax.random.split(jax.random.key(seed), 7)
    src_points = draw_src_points(jax.random.fold_in(key_list[6], 71), 0)
    tgt_points = draw_tgt_points(jax.random.fold_in(key_list[6], 71), 0)
    src_counts = draw_src_counts(jax.random.fold_in(key_list[6], 71), 0)
    tgt_counts = draw_tgt_counts(jax.random.fold_in(key_list[6], 71), 0)
    tile_list = draw_tile_list(jax.random.fold_in(key_list[6], 71), 0)
    tile_count = draw_tile_count(jax.random.fold_in(key_list[6], 71), 0)
    return {"src_points": src_points, "tgt_points": tgt_points, "src_counts": src_counts, "tgt_counts": tgt_counts, "tile_list": tile_list, "tile_count": tile_count}


epsilon = 0.05
very_low = -1e30


def tile_costs(src_blocks, tgt_blocks, src_norms, tgt_norms, rows, cols):
    picked_src = src_blocks[rows]
    picked_tgt = tgt_blocks[cols]
    dots = jnp.einsum('tid,tjd->tij', picked_src, picked_tgt)
    return (src_norms[rows][:, :, None] + tgt_norms[cols][:, None, :] - 2.0 * dots) / picked_src.shape[-1]


def fold_tiles(peak, mass, top, total, owner, used):
    member = (owner[:, None] == jnp.arange(peak.shape[0], dtype=jnp.int32)[None, :]) & used[:, None]
    top = jnp.where(used[:, None], top, very_low)
    candidate = jnp.max(jnp.where(member[:, :, None], top[:, None, :], very_low), axis=0)
    newpeak = jnp.maximum(peak, candidate)
    added = jnp.sum(jnp.where(member[:, :, None], total[:, None, :] * jnp.exp(top[:, None, :] - newpeak[None]), 0.0), axis=0)
    return newpeak, mass * jnp.exp(peak - newpeak) + added


def reference(src_points, tgt_points, src_counts, tgt_counts, tile_list, tile_count):
    src_blocks = src_points.astype(jnp.float32).reshape(ROW_GROUPS, SB_DEV, BLOCK, DIM)
    tgt_blocks = tgt_points.astype(jnp.float32).reshape(COL_GROUPS, TB_DEV, BLOCK, DIM)
    src_norms = jnp.sum(src_blocks * src_blocks, axis=-1)
    tgt_norms = jnp.sum(tgt_blocks * tgt_blocks, axis=-1)
    positions = jnp.arange(BLOCK, dtype=jnp.int32)
    src_valid = (positions[None, :] < src_counts[:, None]).reshape(ROW_GROUPS, SB_DEV, BLOCK)
    tgt_valid = (positions[None, :] < tgt_counts[:, None]).reshape(COL_GROUPS, TB_DEV, BLOCK)
    log_src = jnp.log(jnp.sum(src_counts).astype(jnp.float32))
    log_tgt = jnp.log(jnp.sum(tgt_counts).astype(jnp.float32))
    pair_rows = tile_list.reshape(ROW_GROUPS * COL_GROUPS, TILES_DEV, 2)
    live_rows = tile_count.reshape(ROW_GROUPS * COL_GROUPS)
    devices = jnp.arange(ROW_GROUPS * COL_GROUPS, dtype=jnp.int32)

    def partials(potential, along_rows):
        def device_part(index):
            rowdev = index // COL_GROUPS
            coldev = index % COL_GROUPS
            pairs = pair_rows[index]
            rows = pairs[:, 0]
            cols = pairs[:, 1]
            used = jnp.arange(TILES_DEV, dtype=jnp.int32) < live_rows[index]
            costs = tile_costs(src_blocks[rowdev], tgt_blocks[coldev], src_norms[rowdev], tgt_norms[coldev], rows, cols)
            if along_rows:
                keep = tgt_valid[coldev][cols][:, None, :] & used[:, None, None]
                scores = jnp.where(keep, (potential[coldev][cols][:, None, :] - costs) / epsilon, very_low)
                top = jnp.max(scores, axis=2)
                total = jnp.sum(jnp.exp(scores - top[:, :, None]), axis=2)
                count = SB_DEV
                owner = rows
            else:
                keep = src_valid[rowdev][rows][:, :, None] & used[:, None, None]
                scores = jnp.where(keep, (potential[rowdev][rows][:, :, None] - costs) / epsilon, very_low)
                top = jnp.max(scores, axis=1)
                total = jnp.sum(jnp.exp(scores - top[:, None, :]), axis=1)
                count = TB_DEV
                owner = cols
            start = (jnp.full((count, BLOCK), very_low, jnp.float32), jnp.zeros((count, BLOCK), jnp.float32))
            return fold_tiles(start[0], start[1], top, total, owner, used)
        return lax.map(device_part, devices)

    tgt_pot = jnp.zeros((COL_GROUPS, TB_DEV, BLOCK), jnp.float32)
    src_pot = jnp.zeros((ROW_GROUPS, SB_DEV, BLOCK), jnp.float32)
    for step in range(ITERS):
        peak, mass = partials(tgt_pot, True)
        peak = peak.reshape(ROW_GROUPS, COL_GROUPS, SB_DEV, BLOCK)
        mass = mass.reshape(ROW_GROUPS, COL_GROUPS, SB_DEV, BLOCK)
        whole_peak = jnp.max(peak, axis=1)
        whole_mass = jnp.sum(mass * jnp.exp(peak - whole_peak[:, None]), axis=1)
        src_pot = jnp.where(src_valid, -epsilon * (log_src + whole_peak + jnp.log(whole_mass)), 0.0)
        peak, mass = partials(src_pot, False)
        peak = peak.reshape(ROW_GROUPS, COL_GROUPS, TB_DEV, BLOCK)
        mass = mass.reshape(ROW_GROUPS, COL_GROUPS, TB_DEV, BLOCK)
        whole_peak = jnp.max(peak, axis=0)
        whole_mass = jnp.sum(mass * jnp.exp(peak - whole_peak[None]), axis=0)
        tgt_pot = jnp.where(tgt_valid, -epsilon * (log_tgt + whole_peak + jnp.log(whole_mass)), 0.0)
    return src_pot.reshape(NS), tgt_pot.reshape(NT)
```

```python
import functools
import math

import jax
import jax.numpy as jnp
from jax import lax
from jax.experimental import pallas as pl
from jax.experimental.pallas import tpu as pltpu
from jax.sharding import Mesh, PartitionSpec as P

BLOCK = 256
ITERS = 3
LANES = 128

epsilon = 0.05
very_low = -1e30
DIM = 64
SCALE = 2.0 / (DIM * epsilon) * math.log2(math.e)
INV_SCALE = 1.0 / SCALE


def merged(parts):
    top = jnp.max(parts, axis=0)
    total = jnp.sum(jnp.exp2((parts - top[None]) * SCALE), axis=0)
    return top + jnp.log2(total) * INV_SCALE


def sweep_kernel(side, live_ref, pairs_ref, bias_ref, red_ref, col_ref, out_ref, peak, mass, ta, tb):
    nred = bias_ref.shape[0]
    ncol = out_ref.shape[0]
    bias = bias_ref[...]
    hi = bias.astype(jnp.bfloat16).astype(jnp.float32)
    rest = bias - hi
    mid = rest.astype(jnp.bfloat16).astype(jnp.float32)
    low = rest - mid
    blank = jnp.zeros((DIM, BLOCK), jnp.float32)
    half = DIM // 2
    if nred < half:
        pad = jnp.zeros((half - nred, BLOCK), jnp.float32)
        hi, mid, low = (jnp.concatenate([v, pad], axis=0) for v in (hi, mid, low))
    ta[...] = jnp.concatenate([blank, hi, mid], axis=0).T.astype(jnp.bfloat16)
    tb[...] = jnp.concatenate([low, blank, blank[:half]], axis=0).T.astype(jnp.bfloat16)
    peak[...] = jnp.full(peak.shape, very_low, jnp.float32)
    mass[...] = jnp.zeros(mass.shape, jnp.float32)
    lane = lax.broadcasted_iota(jnp.int32, (1, LANES), 1)

    def tile(t, _):
        red = pairs_ref[2 * t + side]
        col = pairs_ref[2 * t + 1 - side]
        one_a = ((lane == DIM + red) | (lane == DIM + half + red)).astype(jnp.float32).astype(jnp.bfloat16)
        one_b = (lane == red).astype(jnp.float32).astype(jnp.bfloat16)
        lhs = red_ref[pl.ds(pl.multiple_of(red * BLOCK, BLOCK), BLOCK), :] + ta[...]
        rhs = col_ref[pl.ds(pl.multiple_of(col * BLOCK, BLOCK), BLOCK), :] + one_a
        lhs = jnp.concatenate([lhs, tb[...]], axis=1)
        rhs = jnp.concatenate([rhs, jnp.broadcast_to(one_b, (BLOCK, LANES))], axis=1)
        score = lax.dot_general(
            lhs, rhs, (((1,), (1,)), ((), ())), preferred_element_type=jnp.float32
        ).reshape(BLOCK // 8, 8, BLOCK)
        old = peak[col]
        new = jnp.maximum(old, jnp.max(score, axis=0))
        total = jnp.sum(jnp.exp2((score - new[None]) * SCALE), axis=0)
        mass[col] = mass[col] * jnp.exp2((old - new) * SCALE) + total
        peak[col] = new
        return 0

    lax.fori_loop(0, live_ref[0], tile, 0)
    top = jnp.max(peak[...], axis=1, keepdims=True)
    total = jnp.sum(mass[...] * jnp.exp2((peak[...] - top) * SCALE), axis=1)
    top = top.reshape(ncol, BLOCK)
    used = total > 0.0
    out_ref[...] = jnp.where(used, top + jnp.log2(jnp.where(used, total, 1.0)) * INV_SCALE, very_low)


def sweep(side, live, pairs, bias, red, col):
    ncol = col.shape[0] // BLOCK
    smem = pl.BlockSpec(memory_space=pltpu.SMEM)
    vmem = pl.BlockSpec(memory_space=pltpu.VMEM)
    return pl.pallas_call(
        functools.partial(sweep_kernel, side),
        out_shape=jax.ShapeDtypeStruct((ncol, BLOCK), jnp.float32),
        in_specs=[smem, smem, vmem, vmem, vmem],
        out_specs=vmem,
        scratch_shapes=[
            pltpu.VMEM((ncol, 8, BLOCK), jnp.float32),
            pltpu.VMEM((ncol, 8, BLOCK), jnp.float32),
            pltpu.VMEM((BLOCK, LANES), jnp.bfloat16),
            pltpu.VMEM((BLOCK, LANES), jnp.bfloat16),
        ],
        compiler_params=pltpu.CompilerParams(vmem_limit_bytes=24 * 1024 * 1024),
    )(live, pairs, bias, red, col)


def spread(value, axes, count):
    stacked = jnp.broadcast_to(value[None], (count,) + value.shape)
    return lax.all_to_all(stacked, axes, 0, 0)


def on_device(sizes, src_points, tgt_points, src_counts, tgt_counts, tile_list, tile_count):
    src_nblk = src_counts.shape[0]
    tgt_nblk = tgt_counts.shape[0]
    nplane = sizes["x"] * sizes["z"]
    ny = sizes["y"]
    pad = ((0, 0), (0, LANES - DIM))
    src = jnp.pad(src_points, pad)
    tgt = jnp.pad(tgt_points, pad)
    src_norms = jnp.sum(jnp.square(src_points.astype(jnp.float32)), axis=-1).reshape(src_nblk, BLOCK)
    tgt_norms = jnp.sum(jnp.square(tgt_points.astype(jnp.float32)), axis=-1).reshape(tgt_nblk, BLOCK)
    positions = jnp.arange(BLOCK, dtype=jnp.int32)
    src_valid = positions[None, :] < src_counts[:, None]
    tgt_valid = positions[None, :] < tgt_counts[:, None]
    pairs = tile_list.reshape(-1)
    live = tile_count.reshape(-1)
    src_local = jnp.sum(src_counts).astype(jnp.float32)
    tgt_local = jnp.sum(tgt_counts).astype(jnp.float32)
    core = lax.axis_index("core")
    half = tgt_nblk // 2

    tgt_pot = -0.5 * tgt_norms
    for step in range(ITERS):
        bias = jnp.where(tgt_valid, tgt_pot, very_low)
        part = sweep(1, live, pairs, bias, tgt, src)
        if step == 0:
            part = jnp.concatenate([part, jnp.full((8, BLOCK), tgt_local)], axis=0)
        parts = spread(part, "y", ny)
        if step == 0:
            tgt_total = jnp.sum(parts[:, src_nblk, 0])
            parts = parts[:, :src_nblk]
        src_pot = -merged(parts)
        bias = jnp.where(src_valid, src_pot, very_low)
        part = sweep(0, live, pairs, bias, src, tgt)
        if step == 0:
            pair = lax.all_gather(jnp.concatenate([part, jnp.full((8, BLOCK), src_local)], axis=0), "core")
            mine = merged(lax.dynamic_slice_in_dim(pair, core * half, half, 1))
            both = jnp.sum(pair[:, tgt_nblk, 0])
            parts = spread(jnp.concatenate([mine, jnp.full((8, BLOCK), both)], axis=0), ("x", "z"), nplane)
            src_total = jnp.sum(parts[:, half, 0])
            parts = parts[:, :half]
        else:
            pair = lax.all_gather(part, "core")
            mine = merged(lax.dynamic_slice_in_dim(pair, core * half, half, 1))
            parts = spread(mine, ("x", "z"), nplane)
        tgt_pot = -lax.all_gather(merged(parts), "core", axis=0, tiled=True)
    log_src = jnp.log(src_total)
    log_tgt = jnp.log(tgt_total)
    src_shift = -epsilon * (ITERS * log_src - (ITERS - 1) * log_tgt)
    tgt_shift = epsilon * ITERS * (log_src - log_tgt)
    src_out = jnp.where(src_valid, src_pot * (2.0 / DIM) + src_norms * (1.0 / DIM) + src_shift, 0.0)
    tgt_out = jnp.where(tgt_valid, tgt_pot * (2.0 / DIM) + tgt_norms * (1.0 / DIM) + tgt_shift, 0.0)
    return (src_out.reshape(-1), tgt_out.reshape(-1))


def solution(mesh):
    sizes = {"x": 4, "z": 8, "core": 2, "y": mesh.shape["col"]}
    fine = Mesh(mesh.devices.reshape(tuple(sizes.values())), tuple(sizes))
    row = ("x", "z", "core")
    return jax.shard_map(
        functools.partial(on_device, sizes),
        mesh=fine,
        in_specs=(P(row, None), P("y", None), P(row), P("y"), P(row, "y", None, None), P(row, "y")),
        out_specs=(P(row), P("y")),
        check_vma=False,
    )
```

```python
import functools
import math

import jax
import jax.numpy as jnp
from jax import lax
from jax.experimental import pallas as pl
from jax.experimental.pallas import tpu as pltpu
from jax.sharding import Mesh, PartitionSpec as P

BLOCK = 256
ITERS = 3
LANES = 128
GROUP = 8

epsilon = 0.05
very_low = -1e30
DIM = 64
SCALE = 2.0 / (DIM * epsilon) * math.log2(math.e)
INV_SCALE = 1.0 / SCALE

SMEM = pl.BlockSpec(memory_space=pltpu.SMEM)
VMEM = pl.BlockSpec(memory_space=pltpu.VMEM)
PARAMS = pltpu.CompilerParams(vmem_limit_bytes=24 * 1024 * 1024)


def total_count(counts_ref):
    return lax.fori_loop(0, counts_ref.shape[0], lambda i, s: s + counts_ref[i], 0).astype(jnp.float32)


def merged(parts):
    top = jnp.max(parts, axis=0)
    total = jnp.sum(jnp.exp2((parts - top[None]) * SCALE), axis=0)
    return top + jnp.log2(total) * INV_SCALE


def prepare_kernel(counts_s, counts_t, src_t, tgt_t, src, tgt, half_s, half_t, real_s, real_t):
    lane = lax.broadcasted_iota(jnp.int32, (1, LANES), 1)
    for counts, points, out, norms, real in (
        (counts_s, src_t, src, half_s, real_s),
        (counts_t, tgt_t, tgt, half_t, real_t),
    ):
        for row in range(norms.shape[0]):
            chunk = points[:, row * LANES : (row + 1) * LANES].astype(jnp.float32)
            norms[row : row + 1, :] = 0.5 * jnp.sum(chunk * chunk, axis=0, keepdims=True)
            chunk = jnp.concatenate([chunk, jnp.zeros((LANES - DIM, LANES), jnp.float32)], axis=0)
            out[row * LANES : (row + 1) * LANES, :] = chunk.T.astype(jnp.bfloat16)
            slot = lane + (row % 2) * LANES
            real[row : row + 1, :] = (slot < counts[row // 2]).astype(jnp.float32)


def prepare(src_counts, tgt_counts, src_t, tgt_t):
    ns, nt = src_t.shape[1], tgt_t.shape[1]
    rows_s = jax.ShapeDtypeStruct((ns // LANES, LANES), jnp.float32)
    rows_t = jax.ShapeDtypeStruct((nt // LANES, LANES), jnp.float32)
    return pl.pallas_call(
        prepare_kernel,
        out_shape=(
            jax.ShapeDtypeStruct((ns, LANES), jnp.bfloat16),
            jax.ShapeDtypeStruct((nt, LANES), jnp.bfloat16),
            rows_s,
            rows_t,
            rows_s,
            rows_t,
        ),
        in_specs=[SMEM, SMEM, VMEM, VMEM],
        out_specs=(VMEM,) * 6,
        compiler_params=PARAMS,
    )(src_counts, tgt_counts, src_t, tgt_t)


def sweep_kernel(
    side, live_ref, pairs_ref, counts_ref, parts_ref, real_ref, red_ref, col_ref,
    out_ref, rows_in, rows_out, peak, mass, ta, tb,
):
    nred = red_ref.shape[0] // BLOCK
    ncol = col_ref.shape[0] // BLOCK
    if len(parts_ref.shape) == 3:
        value = merged(parts_ref[:, : 2 * nred, :])
    else:
        gap = parts_ref.shape[0] // (2 * nred)
        value = parts_ref[pl.ds(0, 2 * nred, stride=gap), :] if gap > 1 else parts_ref[...]
    rows_in[...] = jnp.where(real_ref[...] > 0.0, -value, very_low)
    bias = jnp.concatenate([rows_in[pl.ds(h, nred, stride=2), :] for h in (0, 1)], axis=1)
    hi = bias.astype(jnp.bfloat16).astype(jnp.float32)
    rest = bias - hi
    mid = rest.astype(jnp.bfloat16).astype(jnp.float32)
    low = rest - mid
    blank = jnp.zeros((DIM, BLOCK), jnp.float32)
    half = DIM // 2
    if nred < half:
        pad = jnp.zeros((half - nred, BLOCK), jnp.float32)
        hi, mid, low = (jnp.concatenate([v, pad], axis=0) for v in (hi, mid, low))
    ta[...] = jnp.concatenate([blank, hi, mid], axis=0).T.astype(jnp.bfloat16)
    tb[...] = jnp.concatenate([low, blank, blank[:half]], axis=0).T.astype(jnp.bfloat16)
    peak[...] = jnp.full(peak.shape, very_low, jnp.float32)
    mass[...] = jnp.zeros(mass.shape, jnp.float32)
    lane = lax.broadcasted_iota(jnp.int32, (1, LANES), 1)
    live = live_ref[0, 0]

    def tile(t):
        red = pairs_ref[side, t]
        col = pairs_ref[1 - side, t]
        slot = jnp.where(t < live, col, ncol)
        one_a = ((lane == DIM + red) | (lane == DIM + half + red)).astype(jnp.float32).astype(jnp.bfloat16)
        one_b = (lane == red).astype(jnp.float32).astype(jnp.bfloat16)
        lhs = red_ref[pl.ds(pl.multiple_of(red * BLOCK, BLOCK), BLOCK), :] + ta[...]
        rhs = col_ref[pl.ds(pl.multiple_of(col * BLOCK, BLOCK), BLOCK), :] + one_a
        lhs = jnp.concatenate([lhs, tb[...]], axis=1)
        rhs = jnp.concatenate([rhs, jnp.broadcast_to(one_b, (BLOCK, LANES))], axis=1)
        score = lax.dot_general(
            lhs, rhs, (((1,), (1,)), ((), ())), preferred_element_type=jnp.float32
        ).reshape(BLOCK // 8, 8, BLOCK)
        old = peak[slot]
        new = jnp.maximum(old, jnp.max(score, axis=0))
        total = jnp.sum(jnp.exp2((score - new[None]) * SCALE), axis=0)
        mass[slot] = mass[slot] * jnp.exp2((old - new) * SCALE) + total
        peak[slot] = new

    def group(i, _):
        for u in range(GROUP):
            tile(i * GROUP + u)
        return 0

    lax.fori_loop(0, (live + GROUP - 1) // GROUP, group, 0)
    tops = peak[:ncol]
    top = jnp.max(tops, axis=1, keepdims=True)
    total = jnp.sum(mass[:ncol] * jnp.exp2((tops - top) * SCALE), axis=1)
    top = top.reshape(ncol, BLOCK)
    used = total > 0.0
    part = jnp.where(used, top + jnp.log2(jnp.where(used, total, 1.0)) * INV_SCALE, very_low)
    for h in (0, 1):
        rows_out[pl.ds(h, ncol, stride=2), :] = part[:, h * LANES : (h + 1) * LANES]
    if len(out_ref.shape) == 2:
        out_ref[...] = rows_out[...]
    else:
        out_ref[:, : 2 * ncol, :] = jnp.broadcast_to(rows_out[...][None], (out_ref.shape[0], 2 * ncol, LANES))
        extra = out_ref.shape[1] - 2 * ncol
        if extra:
            out_ref[:, 2 * ncol :, :] = jnp.full((out_ref.shape[0], extra, LANES), total_count(counts_ref))


def sweep(side, out, live, pairs, counts, parts, real, red, col):
    nred, ncol = red.shape[0] // BLOCK, col.shape[0] // BLOCK
    return pl.pallas_call(
        functools.partial(sweep_kernel, side),
        out_shape=jax.ShapeDtypeStruct(out, jnp.float32),
        in_specs=[SMEM, SMEM, SMEM, VMEM, VMEM, VMEM, VMEM],
        out_specs=VMEM,
        scratch_shapes=[
            pltpu.VMEM((2 * nred, LANES), jnp.float32),
            pltpu.VMEM((2 * ncol, LANES), jnp.float32),
            pltpu.VMEM((ncol + 1, 8, BLOCK), jnp.float32),
            pltpu.VMEM((ncol + 1, 8, BLOCK), jnp.float32),
            pltpu.VMEM((BLOCK, LANES), jnp.bfloat16),
            pltpu.VMEM((BLOCK, LANES), jnp.bfloat16),
        ],
        compiler_params=PARAMS,
    )(live, pairs, counts, parts, real, red, col)


def shard_kernel(counts_ref, parts_ref, out_ref):
    count = parts_ref.shape[0]
    value = jnp.broadcast_to(merged(parts_ref[...])[None], (count, LANES))
    if out_ref.shape[0] == count:
        out_ref[...] = value
    else:
        out_ref[pl.ds(0, count, stride=2), :] = value
        out_ref[pl.ds(1, count, stride=2), :] = jnp.full((count, LANES), total_count(counts_ref))


def shard(counts, parts, rows):
    return pl.pallas_call(
        shard_kernel,
        out_shape=jax.ShapeDtypeStruct((rows, LANES), jnp.float32),
        in_specs=[SMEM, VMEM],
        out_specs=VMEM,
        compiler_params=PARAMS,
    )(counts, parts)


def on_device(rows, cols, src_points, tgt_points, src_counts, tgt_counts, tile_list, tile_count):
    pairs = tile_list.reshape(tile_list.shape[2:]).T
    src, tgt, src_half, tgt_half, src_real, tgt_real = prepare(
        src_counts, tgt_counts, src_points.T, tgt_points.T
    )
    src_rows = src_half.shape[0]
    tgt_rows = tgt_half.shape[0]
    row = ("x", "z", "core")

    tgt_part = tgt_half
    for step in range(ITERS):
        extra = 8 if step == 0 else 0
        src_parts = sweep(
            1, (cols, src_rows + extra, LANES), tile_count, pairs, tgt_counts, tgt_part, tgt_real, tgt, src
        )
        src_parts = lax.all_to_all(src_parts, "y", 0, 0)
        part = sweep(0, (tgt_rows, LANES), tile_count, pairs, src_counts, src_parts, src_real, src, tgt)
        part = lax.all_to_all(part, row, 0, 0, tiled=True)
        part = shard(src_counts, part, 2 * rows if step == 0 else rows)
        tgt_part = lax.all_to_all(part, row, 0, 0, tiled=True)
        if step == 0:
            tgt_total = jnp.sum(src_parts[:, src_rows, 0])
            src_total = jnp.sum(tgt_part.reshape(rows, 2, LANES)[:, 1, 0])
    log_src = jnp.log(src_total)
    log_tgt = jnp.log(tgt_total)
    src_shift = -epsilon * (ITERS * log_src - (ITERS - 1) * log_tgt)
    tgt_shift = epsilon * ITERS * (log_src - log_tgt)
    src_out = jnp.where(src_real > 0.0, (src_half - merged(src_parts)) * (2.0 / DIM) + src_shift, 0.0)
    tgt_out = jnp.where(tgt_real > 0.0, (tgt_half - tgt_part) * (2.0 / DIM) + tgt_shift, 0.0)
    return (src_out.reshape(-1), tgt_out.reshape(-1))


def solution(mesh):
    rows, cols = mesh.shape["row"], mesh.shape["col"]
    fine = Mesh(mesh.devices.reshape(4, 8, 2, cols), ("x", "z", "core", "y"))
    row = ("x", "z", "core")
    return jax.shard_map(
        functools.partial(on_device, rows, cols),
        mesh=fine,
        in_specs=(P(row, None), P("y", None), P(row), P("y"), P(row, "y", None, None), P(row, "y")),
        out_specs=(P(row), P("y")),
        check_vma=False,
    )
```

```python
import functools
import math

import jax
import jax.numpy as jnp
from jax import lax
from jax.experimental import pallas as pl
from jax.experimental.pallas import tpu as pltpu
from jax.sharding import Mesh, PartitionSpec as P

BLOCK = 256
ITERS = 3
LANES = 128
GROUP = 8

epsilon = 0.05
very_low = -1e30
DIM = 64
SCALE = 2.0 / (DIM * epsilon) * math.log2(math.e)
INV_SCALE = 1.0 / SCALE

SMEM = pl.BlockSpec(memory_space=pltpu.SMEM)
HBM = pl.BlockSpec(memory_space=pltpu.HBM)
VMEM = pl.BlockSpec(memory_space=pltpu.VMEM)
PARAMS = pltpu.CompilerParams(vmem_limit_bytes=24 * 1024 * 1024)


def in_hbm(*arrays):
    return [pltpu.with_memory_space_constraint(a, pltpu.HBM) for a in arrays]


def total_count(counts_ref):
    return lax.fori_loop(0, counts_ref.shape[0], lambda i, s: s + counts_ref[i], 0).astype(jnp.float32)


def merged(parts):
    top = jnp.max(parts, axis=0)
    total = jnp.sum(jnp.exp2((parts - top[None]) * SCALE), axis=0)
    return top + jnp.log2(total) * INV_SCALE


def prepare_kernel(counts_s, counts_t, src_t, tgt_t, src, tgt, half_s, half_t, real_s, real_t, cs, ct, xs, xt, sems):
    copies = [
        pltpu.make_async_copy(a, b, sems.at[i])
        for i, (a, b) in enumerate(((counts_s, cs), (src_t, xs), (counts_t, ct), (tgt_t, xt)))
    ]
    for copy in copies:
        copy.start()
    lane = lax.broadcasted_iota(jnp.int32, (1, LANES), 1)
    for side, (counts, points, out, norms, real) in enumerate(
        ((cs, xs, src, half_s, real_s), (ct, xt, tgt, half_t, real_t))
    ):
        copies[2 * side].wait()
        copies[2 * side + 1].wait()
        for row in range(norms.shape[0]):
            chunk = points[:, row * LANES : (row + 1) * LANES].astype(jnp.float32)
            norms[row : row + 1, :] = 0.5 * jnp.sum(chunk * chunk, axis=0, keepdims=True)
            chunk = jnp.concatenate([chunk, jnp.zeros((LANES - DIM, LANES), jnp.float32)], axis=0)
            out[row * LANES : (row + 1) * LANES, :] = chunk.T.astype(jnp.bfloat16)
            slot = lane + (row % 2) * LANES
            real[row : row + 1, :] = (slot < counts[row // 2]).astype(jnp.float32)


def prepare(src_counts, tgt_counts, src_t, tgt_t):
    ns, nt = src_t.shape[1], tgt_t.shape[1]
    rows_s = jax.ShapeDtypeStruct((ns // LANES, LANES), jnp.float32)
    rows_t = jax.ShapeDtypeStruct((nt // LANES, LANES), jnp.float32)
    return pl.pallas_call(
        prepare_kernel,
        out_shape=(
            jax.ShapeDtypeStruct((ns, LANES), jnp.bfloat16),
            jax.ShapeDtypeStruct((nt, LANES), jnp.bfloat16),
            rows_s,
            rows_t,
            rows_s,
            rows_t,
        ),
        in_specs=[HBM] * 4,
        out_specs=(VMEM,) * 6,
        scratch_shapes=[
            pltpu.SMEM(src_counts.shape, jnp.int32),
            pltpu.SMEM(tgt_counts.shape, jnp.int32),
            pltpu.VMEM(src_t.shape, jnp.bfloat16),
            pltpu.VMEM(tgt_t.shape, jnp.bfloat16),
            pltpu.SemaphoreType.DMA((4,)),
        ],
        compiler_params=PARAMS,
    )(*in_hbm(src_counts, tgt_counts, src_t, tgt_t))


def sweep_kernel(
    side, live_ref, pairs_hbm, counts_hbm, parts_ref, real_ref, red_ref, col_ref,
    out_ref, rows_in, rows_out, peak, mass, ta, tb, pairs_ref, counts_ref, sems,
):
    fetches = [
        pltpu.make_async_copy(a, b, sems.at[i])
        for i, (a, b) in enumerate(((pairs_hbm, pairs_ref), (counts_hbm, counts_ref)))
    ]
    for fetch in fetches:
        fetch.start()
    nred = red_ref.shape[0] // BLOCK
    ncol = col_ref.shape[0] // BLOCK
    if len(parts_ref.shape) == 3:
        value = merged(parts_ref[:, : 2 * nred, :])
    else:
        value = parts_ref[...]
    rows_in[...] = jnp.where(real_ref[...] > 0.0, -value, very_low)
    bias = jnp.concatenate([rows_in[pl.ds(h, nred, stride=2), :] for h in (0, 1)], axis=1)
    hi = bias.astype(jnp.bfloat16).astype(jnp.float32)
    rest = bias - hi
    mid = rest.astype(jnp.bfloat16).astype(jnp.float32)
    low = rest - mid
    blank = jnp.zeros((DIM, BLOCK), jnp.float32)
    half = DIM // 2
    if nred < half:
        pad = jnp.zeros((half - nred, BLOCK), jnp.float32)
        hi, mid, low = (jnp.concatenate([v, pad], axis=0) for v in (hi, mid, low))
    ta[...] = jnp.concatenate([blank, hi, mid], axis=0).T.astype(jnp.bfloat16)
    tb[...] = jnp.concatenate([low, blank, blank[:half]], axis=0).T.astype(jnp.bfloat16)
    peak[...] = jnp.full(peak.shape, very_low, jnp.float32)
    mass[...] = jnp.zeros(mass.shape, jnp.float32)
    lane = lax.broadcasted_iota(jnp.int32, (1, LANES), 1)
    for fetch in fetches:
        fetch.wait()
    live = live_ref[0, 0]

    def tile(t):
        red = pairs_ref[side, t]
        col = pairs_ref[1 - side, t]
        slot = jnp.where(t < live, col, ncol)
        one_a = ((lane == DIM + red) | (lane == DIM + half + red)).astype(jnp.float32).astype(jnp.bfloat16)
        one_b = (lane == red).astype(jnp.float32).astype(jnp.bfloat16)
        lhs = red_ref[pl.ds(pl.multiple_of(red * BLOCK, BLOCK), BLOCK), :] + ta[...]
        rhs = col_ref[pl.ds(pl.multiple_of(col * BLOCK, BLOCK), BLOCK), :] + one_a
        lhs = jnp.concatenate([lhs, tb[...]], axis=1)
        rhs = jnp.concatenate([rhs, jnp.broadcast_to(one_b, (BLOCK, LANES))], axis=1)
        score = lax.dot_general(
            lhs, rhs, (((1,), (1,)), ((), ())), preferred_element_type=jnp.float32
        ).reshape(BLOCK // 8, 8, BLOCK)
        old = peak[slot]
        new = jnp.maximum(old, jnp.max(score, axis=0))
        total = jnp.sum(jnp.exp2((score - new[None]) * SCALE), axis=0)
        mass[slot] = mass[slot] * jnp.exp2((old - new) * SCALE) + total
        peak[slot] = new

    def group(i, _):
        for u in range(GROUP):
            tile(i * GROUP + u)
        return 0

    lax.fori_loop(0, (live + GROUP - 1) // GROUP, group, 0)
    tops = peak[:ncol]
    top = jnp.max(tops, axis=1, keepdims=True)
    total = jnp.sum(mass[:ncol] * jnp.exp2((tops - top) * SCALE), axis=1)
    top = top.reshape(ncol, BLOCK)
    used = total > 0.0
    part = jnp.where(used, top + jnp.log2(jnp.where(used, total, 1.0)) * INV_SCALE, very_low)
    for h in (0, 1):
        rows_out[pl.ds(h, ncol, stride=2), :] = part[:, h * LANES : (h + 1) * LANES]
    copies, rows, _ = out_ref.shape
    out_ref[:, : 2 * ncol, :] = jnp.broadcast_to(rows_out[...][None], (copies, 2 * ncol, LANES))
    if rows > 2 * ncol:
        out_ref[:, 2 * ncol :, :] = jnp.full((copies, rows - 2 * ncol, LANES), total_count(counts_ref))


def sweep(side, out, live, pairs, counts, parts, real, red, col):
    nred, ncol = red.shape[0] // BLOCK, col.shape[0] // BLOCK
    return pl.pallas_call(
        functools.partial(sweep_kernel, side),
        out_shape=jax.ShapeDtypeStruct(out, jnp.float32),
        in_specs=[SMEM, HBM, HBM, VMEM, VMEM, VMEM, VMEM],
        out_specs=VMEM,
        scratch_shapes=[
            pltpu.VMEM((2 * nred, LANES), jnp.float32),
            pltpu.VMEM((2 * ncol, LANES), jnp.float32),
            pltpu.VMEM((ncol + 1, 8, BLOCK), jnp.float32),
            pltpu.VMEM((ncol + 1, 8, BLOCK), jnp.float32),
            pltpu.VMEM((BLOCK, LANES), jnp.bfloat16),
            pltpu.VMEM((BLOCK, LANES), jnp.bfloat16),
            pltpu.SMEM(pairs.shape, jnp.int32),
            pltpu.SMEM(counts.shape, jnp.int32),
            pltpu.SemaphoreType.DMA((2,)),
        ],
        compiler_params=PARAMS,
    )(live, *in_hbm(pairs, counts), parts, real, red, col)


def relay_kernel(rows, parts_ref, out_ref):
    copies, height, _ = out_ref.shape
    out_ref[:, :rows, :] = jnp.broadcast_to(merged(parts_ref[:, :rows, :])[None], (copies, rows, LANES))
    if height > rows:
        count = jnp.sum(parts_ref[:, rows:, :], axis=0)
        out_ref[:, rows:, :] = jnp.broadcast_to(count[None], (copies, height - rows, LANES))


def relay(rows, copies, parts):
    return pl.pallas_call(
        functools.partial(relay_kernel, rows),
        out_shape=jax.ShapeDtypeStruct((copies,) + parts.shape[1:], jnp.float32),
        in_specs=[VMEM],
        out_specs=VMEM,
        compiler_params=PARAMS,
    )(parts)


def on_device(sizes, src_points, tgt_points, src_counts, tgt_counts, tile_list, tile_count):
    pairs = tile_list.reshape(tile_list.shape[2:]).T
    src, tgt, src_half, tgt_half, src_real, tgt_real = prepare(
        src_counts, tgt_counts, src_points.T, tgt_points.T
    )
    src_rows = src_half.shape[0]
    tgt_rows = tgt_half.shape[0]

    tgt_parts = tgt_half
    for step in range(ITERS):
        extra = 8 if step == 0 else 0
        out = (sizes["y"], src_rows + extra, LANES)
        src_parts = sweep(1, out, tile_count, pairs, tgt_counts, tgt_parts, tgt_real, tgt, src)
        src_parts = lax.all_to_all(src_parts, "y", 0, 0)
        out = (sizes["z"], tgt_rows + extra, LANES)
        tgt_parts = sweep(0, out, tile_count, pairs, src_counts, src_parts, src_real, src, tgt)
        tgt_parts = lax.all_to_all(tgt_parts, "z", 0, 0)
        tgt_parts = relay(tgt_rows, sizes["x"] * sizes["core"], tgt_parts)
        tgt_parts = lax.all_to_all(tgt_parts, ("x", "core"), 0, 0)
        if step == 0:
            tgt_total = jnp.sum(src_parts[:, src_rows, 0])
            src_total = jnp.sum(tgt_parts[:, tgt_rows, 0])
    log_src = jnp.log(src_total)
    log_tgt = jnp.log(tgt_total)
    src_shift = -epsilon * (ITERS * log_src - (ITERS - 1) * log_tgt)
    tgt_shift = epsilon * ITERS * (log_src - log_tgt)
    src_out = jnp.where(src_real > 0.0, (src_half - merged(src_parts)) * (2.0 / DIM) + src_shift, 0.0)
    tgt_out = jnp.where(tgt_real > 0.0, (tgt_half - merged(tgt_parts)) * (2.0 / DIM) + tgt_shift, 0.0)
    return (src_out.reshape(-1), tgt_out.reshape(-1))


def solution(mesh):
    sizes = {"x": 4, "z": 8, "core": 2, "y": mesh.shape["col"]}
    fine = Mesh(mesh.devices.reshape(tuple(sizes.values())), tuple(sizes))
    row = ("x", "z", "core")
    return jax.shard_map(
        functools.partial(on_device, sizes),
        mesh=fine,
        in_specs=(P(row, None), P("y", None), P(row), P("y"), P(row, "y", None, None), P(row, "y")),
        out_specs=(P(row), P("y")),
        check_vma=False,
    )
```

```python
import functools
import math

import jax
import jax.numpy as jnp
from jax import lax
from jax.experimental import pallas as pl
from jax.experimental.pallas import tpu as pltpu
from jax.sharding import Mesh, PartitionSpec as P

BLOCK = 256
ITERS = 3
LANES = 128
GROUP = 16

epsilon = 0.05
very_low = -1e30
DIM = 64
SCALE = 2.0 / (DIM * epsilon) * math.log2(math.e)
INV_SCALE = 1.0 / SCALE

SMEM = pl.BlockSpec(memory_space=pltpu.SMEM)
HBM = pl.BlockSpec(memory_space=pltpu.HBM)
VMEM = pl.BlockSpec(memory_space=pltpu.VMEM)
PARAMS = pltpu.CompilerParams(vmem_limit_bytes=24 * 1024 * 1024)


def in_hbm(*arrays):
    return [pltpu.with_memory_space_constraint(a, pltpu.HBM) for a in arrays]


def merged(parts):
    top = jnp.max(parts, axis=0)
    total = jnp.sum(jnp.exp2((parts - top[None]) * SCALE), axis=0)
    return top + jnp.log2(total) * INV_SCALE


def prepare_kernel(counts_s, counts_t, src_t, tgt_t, src, tgt, half_s, half_t, real_s, real_t, sum_s, sum_t, cs, ct, xs, xt, sems):
    copies = [
        pltpu.make_async_copy(a, b, sems.at[i])
        for i, (a, b) in enumerate(((counts_s, cs), (src_t, xs), (counts_t, ct), (tgt_t, xt)))
    ]
    for copy in copies:
        copy.start()
    lane = lax.broadcasted_iota(jnp.int32, (1, LANES), 1)
    for side, (counts, points, out, norms, real, total) in enumerate(
        ((cs, xs, src, half_s, real_s, sum_s), (ct, xt, tgt, half_t, real_t, sum_t))
    ):
        copies[2 * side].wait()
        copies[2 * side + 1].wait()
        count = sum(counts[i] for i in range(counts.shape[0]))
        total[...] = jnp.full(total.shape, count).astype(jnp.float32)
        for row in range(norms.shape[0]):
            chunk = points[:, row * LANES : (row + 1) * LANES].astype(jnp.float32)
            norms[row : row + 1, :] = 0.5 * jnp.sum(chunk * chunk, axis=0, keepdims=True)
            chunk = jnp.concatenate([chunk, jnp.zeros((LANES - DIM, LANES), jnp.float32)], axis=0)
            out[row * LANES : (row + 1) * LANES, :] = chunk.T.astype(jnp.bfloat16)
            slot = lane + (row % 2) * LANES
            real[row : row + 1, :] = (slot < counts[row // 2]).astype(jnp.float32)


def prepare(src_counts, tgt_counts, src_t, tgt_t):
    ns, nt = src_t.shape[1], tgt_t.shape[1]
    rows_s = jax.ShapeDtypeStruct((ns // LANES, LANES), jnp.float32)
    rows_t = jax.ShapeDtypeStruct((nt // LANES, LANES), jnp.float32)
    total = jax.ShapeDtypeStruct((8, LANES), jnp.float32)
    return pl.pallas_call(
        prepare_kernel,
        out_shape=(
            jax.ShapeDtypeStruct((ns, LANES), jnp.bfloat16),
            jax.ShapeDtypeStruct((nt, LANES), jnp.bfloat16),
            rows_s,
            rows_t,
            rows_s,
            rows_t,
            total,
            total,
        ),
        in_specs=[HBM] * 4,
        out_specs=(VMEM,) * 8,
        scratch_shapes=[
            pltpu.SMEM(src_counts.shape, jnp.int32),
            pltpu.SMEM(tgt_counts.shape, jnp.int32),
            pltpu.VMEM(src_t.shape, jnp.bfloat16),
            pltpu.VMEM(tgt_t.shape, jnp.bfloat16),
            pltpu.SemaphoreType.DMA((4,)),
        ],
        compiler_params=PARAMS,
    )(*in_hbm(src_counts, tgt_counts, src_t, tgt_t))


def by_block(rows_ref):
    blocks = rows_ref.shape[0] // 2
    return jnp.concatenate([rows_ref[pl.ds(h, blocks, stride=2), :] for h in (0, 1)], axis=1)


def sweep_kernel(
    side, live_ref, pairs_hbm, parts_ref, red_real, last_ref, col_real, total_ref, red_ref, col_ref,
    out_ref, value_ref, rows, shift, seen, peak, mass, ta, tb, pairs_ref, sem,
):
    fetch = pltpu.make_async_copy(pairs_hbm, pairs_ref, sem)
    fetch.start()
    nred = red_ref.shape[0] // BLOCK
    ncol = col_ref.shape[0] // BLOCK
    value_ref[...] = merged(parts_ref[:, : 2 * nred, :]) if len(parts_ref.shape) == 3 else parts_ref[...]
    bias = jnp.where(by_block(red_real) > 0.0, -by_block(value_ref), very_low)
    hi = bias.astype(jnp.bfloat16).astype(jnp.float32)
    rest = bias - hi
    mid = rest.astype(jnp.bfloat16).astype(jnp.float32)
    low = rest - mid
    blank = jnp.zeros((DIM, BLOCK), jnp.float32)
    half = DIM // 2
    if nred < half:
        pad = jnp.zeros((half - nred, BLOCK), jnp.float32)
        hi, mid, low = (jnp.concatenate([v, pad], axis=0) for v in (hi, mid, low))
    ta[...] = jnp.concatenate([blank, hi, mid], axis=0).T.astype(jnp.bfloat16)
    tb[...] = jnp.concatenate([low, blank, blank[:half]], axis=0).T.astype(jnp.bfloat16)
    lane = lax.broadcasted_iota(jnp.int32, (1, LANES), 1)
    real = by_block(col_real) > 0.0
    shift[...] = jnp.where(real, by_block(last_ref), 0.0)
    seen[...] = jnp.zeros(seen.shape, jnp.float32)
    mass[...] = jnp.zeros(mass.shape, jnp.float32)
    fetch.wait()
    live = live_ref[0, 0]

    def scores(t):
        red = pairs_ref[side, t]
        col = pairs_ref[1 - side, t]
        one_a = ((lane == DIM + red) | (lane == DIM + half + red)).astype(jnp.float32).astype(jnp.bfloat16)
        one_b = (lane == red).astype(jnp.float32).astype(jnp.bfloat16)
        lhs = red_ref[pl.ds(pl.multiple_of(red * BLOCK, BLOCK), BLOCK), :] + ta[...]
        rhs = col_ref[pl.ds(pl.multiple_of(col * BLOCK, BLOCK), BLOCK), :] + one_a
        lhs = jnp.concatenate([lhs, tb[...]], axis=1)
        rhs = jnp.concatenate([rhs, jnp.broadcast_to(one_b, (BLOCK, LANES))], axis=1)
        score = lax.dot_general(lhs, rhs, (((1,), (1,)), ((), ())), preferred_element_type=jnp.float32)
        return score.reshape(BLOCK // 8, 8, BLOCK), col, jnp.where(t < live, col, ncol)

    def tile(t):
        score, col, slot = scores(t)
        terms = jnp.exp2((score - shift[pl.ds(col, 1), :][None]) * SCALE)
        mass[slot] = mass[slot] + jnp.sum(terms, axis=0)
        seen[pl.ds(slot, 1), :] = jnp.ones((1, LANES), jnp.float32)

    def group(i, _):
        for u in range(GROUP):
            tile(i * GROUP + u)
        return 0

    lax.fori_loop(0, (live + GROUP - 1) // GROUP, group, 0)

    def finish(part):
        for h in (0, 1):
            rows[pl.ds(h, ncol, stride=2), :] = part[:, h * LANES : (h + 1) * LANES]
        copies, height, _ = out_ref.shape
        out_ref[:, : 2 * ncol, :] = jnp.broadcast_to(rows[...][None], (copies, 2 * ncol, LANES))
        if height > 2 * ncol:
            out_ref[:, 2 * ncol :, :] = jnp.broadcast_to(total_ref[...][None], (copies, height - 2 * ncol, LANES))

    total = jnp.sum(mass[:ncol], axis=1)
    good = (total > 1e-27) & (total < 1e30)
    finish(jnp.where(good, shift[...] + jnp.log2(jnp.where(good, total, 1.0)) * INV_SCALE, very_low))
    used = jnp.concatenate([seen[:ncol, :]] * 2, axis=1) > 0.0
    lost = jnp.max(jnp.where(used & real & jnp.logical_not(good), 1.0, 0.0))

    @pl.when(lost > 0.0)
    def _():
        peak[...] = jnp.full(peak.shape, very_low, jnp.float32)
        mass[...] = jnp.zeros(mass.shape, jnp.float32)

        def exact(t, _):
            score, _, slot = scores(t)
            old = peak[slot]
            new = jnp.maximum(old, jnp.max(score, axis=0))
            terms = jnp.exp2((score - new[None]) * SCALE)
            mass[slot] = mass[slot] * jnp.exp2((old - new) * SCALE) + jnp.sum(terms, axis=0)
            peak[slot] = new
            return 0

        lax.fori_loop(0, live, exact, 0)
        tops = peak[:ncol]
        top = jnp.max(tops, axis=1, keepdims=True)
        total = jnp.sum(mass[:ncol] * jnp.exp2((tops - top) * SCALE), axis=1)
        some = total > 0.0
        finish(
            jnp.where(
                some, top.reshape(ncol, BLOCK) + jnp.log2(jnp.where(some, total, 1.0)) * INV_SCALE, very_low
            )
        )


def sweep(side, out, live, pairs, parts, red_real, last, col_real, total, red, col):
    nred, ncol = red.shape[0] // BLOCK, col.shape[0] // BLOCK
    return pl.pallas_call(
        functools.partial(sweep_kernel, side),
        out_shape=(
            jax.ShapeDtypeStruct(out, jnp.float32),
            jax.ShapeDtypeStruct((2 * nred, LANES), jnp.float32),
        ),
        in_specs=[SMEM, HBM] + [VMEM] * 7,
        out_specs=(VMEM, VMEM),
        scratch_shapes=[
            pltpu.VMEM((2 * ncol, LANES), jnp.float32),
            pltpu.VMEM((ncol, BLOCK), jnp.float32),
            pltpu.VMEM((ncol + 8, LANES), jnp.float32),
            pltpu.VMEM((ncol + 1, 8, BLOCK), jnp.float32),
            pltpu.VMEM((ncol + 1, 8, BLOCK), jnp.float32),
            pltpu.VMEM((BLOCK, LANES), jnp.bfloat16),
            pltpu.VMEM((BLOCK, LANES), jnp.bfloat16),
            pltpu.SMEM(pairs.shape, jnp.int32),
            pltpu.SemaphoreType.DMA,
        ],
        compiler_params=PARAMS,
    )(live, *in_hbm(pairs), parts, red_real, last, col_real, total, red, col)


def relay_kernel(rows, parts_ref, out_ref):
    copies, height, _ = out_ref.shape
    out_ref[:, :rows, :] = jnp.broadcast_to(merged(parts_ref[:, :rows, :])[None], (copies, rows, LANES))
    if height > rows:
        count = jnp.sum(parts_ref[:, rows:, :], axis=0)
        out_ref[:, rows:, :] = jnp.broadcast_to(count[None], (copies, height - rows, LANES))


def relay(rows, copies, parts):
    return pl.pallas_call(
        functools.partial(relay_kernel, rows),
        out_shape=jax.ShapeDtypeStruct((copies,) + parts.shape[1:], jnp.float32),
        in_specs=[VMEM],
        out_specs=VMEM,
        compiler_params=PARAMS,
    )(parts)


def finish_kernel(
    src_value, src_half, src_real, tgt_parts, tgt_half, tgt_real, first_src, first_tgt, src_out, tgt_out
):
    log_tgt = jnp.log(jnp.sum(first_src[:, src_half.shape[0] :, :], axis=0)[:1])
    log_src = jnp.log(jnp.sum(first_tgt[:, tgt_half.shape[0] :, :], axis=0)[:1])
    src_shift = -epsilon * (ITERS * log_src - (ITERS - 1) * log_tgt)
    tgt_shift = epsilon * ITERS * (log_src - log_tgt)
    for half, value, shift, real, out in (
        (src_half, src_value[...], src_shift, src_real, src_out),
        (tgt_half, merged(tgt_parts[...]), tgt_shift, tgt_real, tgt_out),
    ):
        out[...] = jnp.where(real[...] > 0.0, (half[...] - value) * (2.0 / DIM) + shift, 0.0)


def finish(src_value, src_half, src_real, tgt_parts, tgt_half, tgt_real, first_src, first_tgt):
    return pl.pallas_call(
        finish_kernel,
        out_shape=(
            jax.ShapeDtypeStruct(src_half.shape, jnp.float32),
            jax.ShapeDtypeStruct(tgt_half.shape, jnp.float32),
        ),
        in_specs=[VMEM] * 8,
        out_specs=(VMEM, VMEM),
        compiler_params=PARAMS,
    )(src_value, src_half, src_real, tgt_parts, tgt_half, tgt_real, first_src, first_tgt)


def on_device(sizes, src_points, tgt_points, src_counts, tgt_counts, tile_list, tile_count):
    pairs = tile_list.reshape(tile_list.shape[2:]).T
    src, tgt, src_half, tgt_half, src_real, tgt_real, src_total, tgt_total = prepare(
        src_counts, tgt_counts, src_points.T, tgt_points.T
    )
    src_rows = src_half.shape[0]
    tgt_rows = tgt_half.shape[0]

    tgt_parts = tgt_half
    src_value = src_half
    first = []
    for step in range(ITERS):
        extra = src_total.shape[0] if step == 0 else 0
        out = (sizes["y"], src_rows + extra, LANES)
        src_parts, tgt_value = sweep(
            1, out, tile_count, pairs, tgt_parts, tgt_real, src_value, src_real, tgt_total, tgt, src
        )
        src_parts = lax.all_to_all(src_parts, "y", 0, 0)
        out = (sizes["z"], tgt_rows + extra, LANES)
        tgt_parts, src_value = sweep(
            0, out, tile_count, pairs, src_parts, src_real, tgt_value, tgt_real, src_total, src, tgt
        )
        tgt_parts = lax.all_to_all(tgt_parts, "z", 0, 0)
        tgt_parts = relay(tgt_rows, sizes["x"] * sizes["core"], tgt_parts)
        tgt_parts = lax.all_to_all(tgt_parts, ("x", "core"), 0, 0)
        if step == 0:
            first = [src_parts, tgt_parts]
    src_out, tgt_out = finish(src_value, src_half, src_real, tgt_parts, tgt_half, tgt_real, *first)
    return (src_out.reshape(-1), tgt_out.reshape(-1))


def solution(mesh):
    sizes = {"x": 4, "z": 8, "core": 2, "y": mesh.shape["col"]}
    fine = Mesh(mesh.devices.reshape(tuple(sizes.values())), tuple(sizes))
    row = ("x", "z", "core")
    return jax.shard_map(
        functools.partial(on_device, sizes),
        mesh=fine,
        in_specs=(P(row, None), P("y", None), P(row), P("y"), P(row, "y", None, None), P(row, "y")),
        out_specs=(P(row), P("y")),
        check_vma=False,
    )
```

```python
import functools
import math

import jax
import jax.numpy as jnp
from jax import lax
from jax.experimental import pallas as pl
from jax.experimental.pallas import tpu as pltpu
from jax.sharding import Mesh, PartitionSpec as P

BLOCK = 256
ITERS = 3
LANES = 128
GROUP = 48
PART = 16

epsilon = 0.05
very_low = -1e30
DIM = 64
SCALE = 2.0 / (DIM * epsilon) * math.log2(math.e)
INV_SCALE = 1.0 / SCALE

SMEM = pl.BlockSpec(memory_space=pltpu.SMEM)
HBM = pl.BlockSpec(memory_space=pltpu.HBM)
VMEM = pl.BlockSpec(memory_space=pltpu.VMEM)
PARAMS = pltpu.CompilerParams(vmem_limit_bytes=24 * 1024 * 1024)


def in_hbm(*arrays):
    return [pltpu.with_memory_space_constraint(a, pltpu.HBM) for a in arrays]


def merged(parts):
    top = jnp.max(parts, axis=0)
    total = jnp.sum(jnp.exp2((parts - top[None]) * SCALE), axis=0)
    return top + jnp.log2(total) * INV_SCALE


def prepare_kernel(counts_s, counts_t, src_t, tgt_t, pairs_in, src, tgt, half_s, half_t, real_s, real_t, sum_s, sum_t, pairs_out, xs, xt, cs, ct, sems):
    copies = [
        pltpu.make_async_copy(a, b, sems.at[i])
        for i, (a, b) in enumerate(((counts_s, cs), (src_t, xs), (counts_t, ct), (tgt_t, xt), (pairs_in, pairs_out)))
    ]
    for copy in copies:
        copy.start()
    lane = lax.broadcasted_iota(jnp.int32, (1, LANES), 1)
    for side, (counts, points, out, norms, real, total) in enumerate(
        ((cs, xs, src, half_s, real_s, sum_s), (ct, xt, tgt, half_t, real_t, sum_t))
    ):
        copies[2 * side].wait()
        copies[2 * side + 1].wait()
        count = sum(counts[i] for i in range(counts.shape[0]))
        total[...] = jnp.full(total.shape, count).astype(jnp.float32)
        for row in range(norms.shape[0]):
            chunk = points[:, row * LANES : (row + 1) * LANES].astype(jnp.float32)
            norms[row : row + 1, :] = 0.5 * jnp.sum(chunk * chunk, axis=0, keepdims=True)
            chunk = jnp.concatenate([chunk, jnp.zeros((LANES - DIM, LANES), jnp.float32)], axis=0)
            out[row * LANES : (row + 1) * LANES, :] = chunk.T.astype(jnp.bfloat16)
            slot = lane + (row % 2) * LANES
            real[row : row + 1, :] = (slot < counts[row // 2]).astype(jnp.float32)
    copies[4].wait()


def prepare(src_counts, tgt_counts, src_t, tgt_t, pairs):
    ns, nt = src_t.shape[1], tgt_t.shape[1]
    rows_s = jax.ShapeDtypeStruct((ns // LANES, LANES), jnp.float32)
    rows_t = jax.ShapeDtypeStruct((nt // LANES, LANES), jnp.float32)
    total = jax.ShapeDtypeStruct((8, LANES), jnp.float32)
    return pl.pallas_call(
        prepare_kernel,
        out_shape=(
            jax.ShapeDtypeStruct((ns, LANES), jnp.bfloat16),
            jax.ShapeDtypeStruct((nt, LANES), jnp.bfloat16),
            rows_s,
            rows_t,
            rows_s,
            rows_t,
            total,
            total,
            jax.ShapeDtypeStruct(pairs.shape, jnp.int32),
            jax.ShapeDtypeStruct(src_t.shape, jnp.bfloat16),
            jax.ShapeDtypeStruct(tgt_t.shape, jnp.bfloat16),
        ),
        in_specs=[HBM] * 5,
        out_specs=(VMEM,) * 11,
        scratch_shapes=[
            pltpu.SMEM(src_counts.shape, jnp.int32),
            pltpu.SMEM(tgt_counts.shape, jnp.int32),
            pltpu.SemaphoreType.DMA((5,)),
        ],
        compiler_params=PARAMS,
    )(*in_hbm(src_counts, tgt_counts, src_t, tgt_t, pairs))


def split(value):
    hi = value.astype(jnp.bfloat16).astype(jnp.float32)
    rest = value - hi
    mid = rest.astype(jnp.bfloat16).astype(jnp.float32)
    return hi, mid, rest - mid


def by_block(rows_ref):
    blocks = rows_ref.shape[0] // 2
    return jnp.concatenate([rows_ref[pl.ds(h, blocks, stride=2), :] for h in (0, 1)], axis=1)


def sweep_kernel(
    side, live_ref, pairs_hbm, parts_ref, red_real, last_ref, col_real, total_ref, red_ref, col_ref,
    out_ref, value_ref, rows, shift, seen, peak, mass, columns, shifts, pairs_ref, sem,
):
    fetch = pltpu.make_async_copy(pairs_hbm, pairs_ref, sem)
    fetch.start()
    nred = red_ref.shape[0] // BLOCK
    ncol = col_ref.shape[1] // BLOCK
    value_ref[...] = merged(parts_ref[:, : 2 * nred, :]) if len(parts_ref.shape) == 3 else parts_ref[...]
    bias = jnp.where(by_block(red_real) > 0.0, -by_block(value_ref), very_low)
    hi, mid, low = split(bias)
    for i in range(nred // PART):
        own = slice(i * PART, (i + 1) * PART)
        ones = (lax.broadcasted_iota(jnp.int32, (PART, BLOCK), 0) < 3).astype(jnp.float32)
        pieces = [jnp.zeros((DIM, BLOCK), jnp.float32), hi[own], mid[own], low[own], ones]
        columns[i] = jnp.concatenate(pieces, axis=0).T.astype(jnp.bfloat16)
    lane = lax.broadcasted_iota(jnp.int32, (3 * PART, 1), 0)
    real = by_block(col_real) > 0.0
    last = jnp.where(real, by_block(last_ref), 0.0)
    shift[...] = last
    lower = split(-last)
    row = lax.broadcasted_iota(jnp.int32, (PART, BLOCK), 0)
    for c in range(ncol):
        chunk = jnp.zeros((PART, BLOCK), jnp.float32)
        for i in range(3):
            chunk = jnp.where(row == i, lower[i][c : c + 1, :], chunk)
        shifts[c] = chunk.astype(jnp.bfloat16)
    seen[...] = jnp.zeros(seen.shape, jnp.float32)
    mass[...] = jnp.zeros(mass.shape, jnp.float32)
    fetch.wait()
    live = live_ref[0, 0]

    def scores(t):
        red = pairs_ref[side, t]
        col = pairs_ref[1 - side, t]
        place = lane - (red & (PART - 1))
        ones = ((place == 0) | (place == PART) | (place == 2 * PART)).astype(jnp.float32).astype(jnp.bfloat16)
        ones = jnp.broadcast_to(ones, (3 * PART, BLOCK))
        lhs = red_ref[pl.ds(pl.multiple_of(red * BLOCK, BLOCK), BLOCK), :] + columns[red // PART]
        rhs = col_ref[:, pl.ds(pl.multiple_of(col * BLOCK, BLOCK), BLOCK)]
        rhs = jnp.concatenate([rhs, ones, shifts[col]], axis=0)
        score = jnp.dot(lhs, rhs, preferred_element_type=jnp.float32)
        return score.reshape(BLOCK // 8, 8, BLOCK), col, jnp.where(t < live, col, ncol)

    def tile(t):
        score, col, slot = scores(t)
        terms = jnp.exp2(score * SCALE)
        mass[slot] = mass[slot] + jnp.sum(terms, axis=0)
        seen[pl.ds(slot, 1), :] = jnp.ones((1, LANES), jnp.float32)

    def group(i, _):
        for u in range(GROUP):
            tile(i * GROUP + u)
        return 0

    lax.fori_loop(0, (live + GROUP - 1) // GROUP, group, 0)

    def finish(part):
        for h in (0, 1):
            rows[pl.ds(h, ncol, stride=2), :] = part[:, h * LANES : (h + 1) * LANES]
        copies, height, _ = out_ref.shape
        out_ref[:, : 2 * ncol, :] = jnp.broadcast_to(rows[...][None], (copies, 2 * ncol, LANES))
        if height > 2 * ncol:
            out_ref[:, 2 * ncol :, :] = jnp.broadcast_to(total_ref[...][None], (copies, height - 2 * ncol, LANES))

    total = jnp.sum(mass[:ncol], axis=1)
    good = (total > 1e-27) & (total < 1e30)
    finish(jnp.where(good, shift[...] + jnp.log2(jnp.where(good, total, 1.0)) * INV_SCALE, very_low))
    used = jnp.concatenate([seen[:ncol, :]] * 2, axis=1) > 0.0
    lost = jnp.max(jnp.where(used & real & jnp.logical_not(good), 1.0, 0.0))

    @pl.when(lost > 0.0)
    def _():
        peak[...] = jnp.full(peak.shape, very_low, jnp.float32)
        mass[...] = jnp.zeros(mass.shape, jnp.float32)

        def exact(t, _):
            score, _, slot = scores(t)
            old = peak[slot]
            new = jnp.maximum(old, jnp.max(score, axis=0))
            terms = jnp.exp2((score - new[None]) * SCALE)
            mass[slot] = mass[slot] * jnp.exp2((old - new) * SCALE) + jnp.sum(terms, axis=0)
            peak[slot] = new
            return 0

        lax.fori_loop(0, live, exact, 0)
        tops = peak[:ncol]
        top = jnp.max(tops, axis=1, keepdims=True)
        total = jnp.sum(mass[:ncol] * jnp.exp2((tops - top) * SCALE), axis=1)
        some = total > 0.0
        finish(
            jnp.where(
                some, shift[...] + top.reshape(ncol, BLOCK) + jnp.log2(jnp.where(some, total, 1.0)) * INV_SCALE, very_low
            )
        )


def sweep(side, out, live, pairs, parts, red_real, last, col_real, total, red, col):
    nred, ncol = red.shape[0] // BLOCK, col.shape[1] // BLOCK
    return pl.pallas_call(
        functools.partial(sweep_kernel, side),
        out_shape=(
            jax.ShapeDtypeStruct(out, jnp.float32),
            jax.ShapeDtypeStruct((2 * nred, LANES), jnp.float32),
        ),
        in_specs=[SMEM] + [VMEM] * 8,
        out_specs=(VMEM, VMEM),
        scratch_shapes=[
            pltpu.VMEM((2 * ncol, LANES), jnp.float32),
            pltpu.VMEM((ncol, BLOCK), jnp.float32),
            pltpu.VMEM((ncol + 8, LANES), jnp.float32),
            pltpu.VMEM((ncol + 1, 8, BLOCK), jnp.float32),
            pltpu.VMEM((ncol + 1, 8, BLOCK), jnp.float32),
            pltpu.VMEM((nred // PART, BLOCK, LANES), jnp.bfloat16),
            pltpu.VMEM((ncol, PART, BLOCK), jnp.bfloat16),
            pltpu.SMEM(pairs.shape, jnp.int32),
            pltpu.SemaphoreType.DMA,
        ],
        compiler_params=PARAMS,
    )(live, pairs, parts, red_real, last, col_real, total, red, col)


def relay_kernel(rows, parts_ref, out_ref):
    copies, height, _ = out_ref.shape
    out_ref[:, :rows, :] = jnp.broadcast_to(merged(parts_ref[:, :rows, :])[None], (copies, rows, LANES))
    if height > rows:
        count = jnp.sum(parts_ref[:, rows:, :], axis=0)
        out_ref[:, rows:, :] = jnp.broadcast_to(count[None], (copies, height - rows, LANES))


def relay(rows, copies, parts):
    return pl.pallas_call(
        functools.partial(relay_kernel, rows),
        out_shape=jax.ShapeDtypeStruct((copies,) + parts.shape[1:], jnp.float32),
        in_specs=[VMEM],
        out_specs=VMEM,
        compiler_params=PARAMS,
    )(parts)


def finish_kernel(
    src_value, src_half, src_real, tgt_parts, tgt_half, tgt_real, first_src, first_tgt, src_out, tgt_out
):
    log_tgt = jnp.log(jnp.sum(first_src[:, src_half.shape[0] :, :], axis=0)[:1])
    log_src = jnp.log(jnp.sum(first_tgt[:, tgt_half.shape[0] :, :], axis=0)[:1])
    src_shift = -epsilon * (ITERS * log_src - (ITERS - 1) * log_tgt)
    tgt_shift = epsilon * ITERS * (log_src - log_tgt)
    for half, value, shift, real, out in (
        (src_half, src_value[...], src_shift, src_real, src_out),
        (tgt_half, merged(tgt_parts[...]), tgt_shift, tgt_real, tgt_out),
    ):
        out[...] = jnp.where(real[...] > 0.0, (half[...] - value) * (2.0 / DIM) + shift, 0.0)


def finish(src_value, src_half, src_real, tgt_parts, tgt_half, tgt_real, first_src, first_tgt):
    return pl.pallas_call(
        finish_kernel,
        out_shape=(
            jax.ShapeDtypeStruct(src_half.shape, jnp.float32),
            jax.ShapeDtypeStruct(tgt_half.shape, jnp.float32),
        ),
        in_specs=[VMEM] * 8,
        out_specs=(VMEM, VMEM),
        compiler_params=PARAMS,
    )(src_value, src_half, src_real, tgt_parts, tgt_half, tgt_real, first_src, first_tgt)


def on_device(sizes, src_points, tgt_points, src_counts, tgt_counts, tile_list, tile_count):
    pairs = tile_list.reshape(tile_list.shape[2:]).T
    src, tgt, src_half, tgt_half, src_real, tgt_real, src_total, tgt_total, pairs, src_t, tgt_t = prepare(
        src_counts, tgt_counts, src_points.T, tgt_points.T, pairs
    )
    src_rows = src_half.shape[0]
    tgt_rows = tgt_half.shape[0]

    tgt_parts = tgt_half
    src_value = src_half
    first = []
    for step in range(ITERS):
        extra = src_total.shape[0] if step == 0 else 0
        out = (sizes["y"], src_rows + extra, LANES)
        src_parts, tgt_value = sweep(
            1, out, tile_count, pairs, tgt_parts, tgt_real, src_value, src_real, tgt_total, tgt, src_t
        )
        src_parts = lax.all_to_all(src_parts, "y", 0, 0)
        out = (sizes["z"], tgt_rows + extra, LANES)
        tgt_parts, src_value = sweep(
            0, out, tile_count, pairs, src_parts, src_real, tgt_value, tgt_real, src_total, src, tgt_t
        )
        tgt_parts = lax.all_to_all(tgt_parts, "z", 0, 0)
        tgt_parts = relay(tgt_rows, sizes["x"] * sizes["core"], tgt_parts)
        tgt_parts = lax.all_to_all(tgt_parts, ("x", "core"), 0, 0)
        if step == 0:
            first = [src_parts, tgt_parts]
    src_out, tgt_out = finish(src_value, src_half, src_real, tgt_parts, tgt_half, tgt_real, *first)
    return (src_out.reshape(-1), tgt_out.reshape(-1))


def solution(mesh):
    sizes = {"x": 4, "z": 8, "core": 2, "y": mesh.shape["col"]}
    fine = Mesh(mesh.devices.reshape(tuple(sizes.values())), tuple(sizes))
    row = ("x", "z", "core")
    return jax.shard_map(
        functools.partial(on_device, sizes),
        mesh=fine,
        in_specs=(P(row, None), P("y", None), P(row), P("y"), P(row, "y", None, None), P(row, "y")),
        out_specs=(P(row), P("y")),
        check_vma=False,
    )
```

```python
import functools
import math

import jax
import jax.numpy as jnp
from jax import lax
from jax.experimental import pallas as pl
from jax.experimental.pallas import tpu as pltpu
from jax.sharding import Mesh, PartitionSpec as P

BLOCK = 256
ITERS = 3
LANES = 128
PART = 16
TILE_BITS = 8
TILE_BASE = 1 << TILE_BITS

epsilon = 0.05
very_low = -1e30
DIM = 64
SCALE = 2.0 / (DIM * epsilon) * math.log2(math.e)
INV_SCALE = 1.0 / SCALE

SMEM = pl.BlockSpec(memory_space=pltpu.SMEM)
HBM = pl.BlockSpec(memory_space=pltpu.HBM)
VMEM = pl.BlockSpec(memory_space=pltpu.VMEM)
PARAMS = pltpu.CompilerParams(vmem_limit_bytes=24 * 1024 * 1024)


def in_hbm(*arrays):
    return [pltpu.with_memory_space_constraint(a, pltpu.HBM) for a in arrays]


def merged(parts):
    top = jnp.max(parts, axis=0)
    total = jnp.sum(jnp.exp2((parts - top[None]) * SCALE), axis=0)
    return top + jnp.log2(total) * INV_SCALE


def prepare_kernel(counts_s, counts_t, src_t, tgt_t, pairs_in, src, tgt, half_s, half_t, real_s, real_t, sum_s, sum_t, tiles, xs, xt, cs, ct, pairs, sems):
    copies = [
        pltpu.make_async_copy(a, b, sems.at[i])
        for i, (a, b) in enumerate(((counts_s, cs), (src_t, xs), (counts_t, ct), (tgt_t, xt), (pairs_in, pairs)))
    ]
    for copy in copies:
        copy.start()
    lane = lax.broadcasted_iota(jnp.int32, (1, LANES), 1)
    for side, (counts, points, out, norms, real, total) in enumerate(
        ((cs, xs, src, half_s, real_s, sum_s), (ct, xt, tgt, half_t, real_t, sum_t))
    ):
        copies[2 * side].wait()
        copies[2 * side + 1].wait()
        count = sum(counts[i] for i in range(counts.shape[0]))
        total[...] = jnp.full(total.shape, count).astype(jnp.float32)
        for row in range(norms.shape[0]):
            chunk = points[:, row * LANES : (row + 1) * LANES].astype(jnp.float32)
            norms[row : row + 1, :] = 0.5 * jnp.sum(chunk * chunk, axis=0, keepdims=True)
            chunk = jnp.concatenate([chunk, jnp.zeros((LANES - DIM, LANES), jnp.float32)], axis=0)
            out[row * LANES : (row + 1) * LANES, :] = chunk.T.astype(jnp.bfloat16)
            slot = lane + (row % 2) * LANES
            real[row : row + 1, :] = (slot < counts[row // 2]).astype(jnp.float32)
    copies[4].wait()
    tiles[...] = pairs[:1, :] * TILE_BASE + pairs[1:, :]


def prepare(src_counts, tgt_counts, src_t, tgt_t, pairs):
    ns, nt = src_t.shape[1], tgt_t.shape[1]
    rows_s = jax.ShapeDtypeStruct((ns // LANES, LANES), jnp.float32)
    rows_t = jax.ShapeDtypeStruct((nt // LANES, LANES), jnp.float32)
    total = jax.ShapeDtypeStruct((8, LANES), jnp.float32)
    return pl.pallas_call(
        prepare_kernel,
        out_shape=(
            jax.ShapeDtypeStruct((ns, LANES), jnp.bfloat16),
            jax.ShapeDtypeStruct((nt, LANES), jnp.bfloat16),
            rows_s,
            rows_t,
            rows_s,
            rows_t,
            total,
            total,
            jax.ShapeDtypeStruct((1, pairs.shape[1]), jnp.int32),
            jax.ShapeDtypeStruct(src_t.shape, jnp.bfloat16),
            jax.ShapeDtypeStruct(tgt_t.shape, jnp.bfloat16),
        ),
        in_specs=[HBM] * 5,
        out_specs=(VMEM,) * 11,
        scratch_shapes=[
            pltpu.SMEM(src_counts.shape, jnp.int32),
            pltpu.SMEM(tgt_counts.shape, jnp.int32),
            pltpu.VMEM(pairs.shape, jnp.int32),
            pltpu.SemaphoreType.DMA((5,)),
        ],
        compiler_params=PARAMS,
    )(*in_hbm(src_counts, tgt_counts, src_t, tgt_t, pairs))


def whole(parts_ref, rows):
    count, height, _ = parts_ref.shape
    if height >= rows:
        return merged(parts_ref[:, :rows, :])
    half = rows // 2
    return jnp.concatenate(
        [merged(jnp.stack([parts_ref[i, :half, :] for i in range(c, count, 2)])) for c in (0, 1)], axis=0
    )


def split(value):
    hi = value.astype(jnp.bfloat16).astype(jnp.float32)
    rest = value - hi
    mid = rest.astype(jnp.bfloat16).astype(jnp.float32)
    return hi, mid, rest - mid


def by_block(rows_ref):
    blocks = rows_ref.shape[0] // 2
    return jnp.concatenate([rows_ref[pl.ds(h, blocks, stride=2), :] for h in (0, 1)], axis=1)


def sweep_kernel(
    side, live_ref, tiles_ref, parts_ref, red_real, last_ref, col_real, total_ref, red_ref, col_ref,
    out_ref, value_ref, rows, shift, seen, peak, mass, columns, shifts, pairs_ref, sem,
):
    nred = red_ref.shape[0] // BLOCK
    ncol = col_ref.shape[1] // BLOCK
    value_ref[...] = whole(parts_ref, 2 * nred) if len(parts_ref.shape) == 3 else parts_ref[...]
    bias = jnp.where(by_block(red_real) > 0.0, -by_block(value_ref), very_low)
    hi, mid, low = split(bias)
    for i in range(nred // PART):
        own = slice(i * PART, (i + 1) * PART)
        ones = (lax.broadcasted_iota(jnp.int32, (PART, BLOCK), 0) < 3).astype(jnp.float32)
        pieces = [jnp.zeros((DIM, BLOCK), jnp.float32), hi[own], mid[own], low[own], ones]
        columns[i] = jnp.concatenate(pieces, axis=0).T.astype(jnp.bfloat16)
    lane = lax.broadcasted_iota(jnp.int32, (3 * PART, 1), 0)
    real = by_block(col_real) > 0.0
    last = jnp.where(real, by_block(last_ref), 0.0)
    shift[...] = last
    lower = split(-last)
    row = lax.broadcasted_iota(jnp.int32, (PART, BLOCK), 0)
    for c in range(ncol):
        chunk = jnp.zeros((PART, BLOCK), jnp.float32)
        for i in range(3):
            chunk = jnp.where(row == i, lower[i][c : c + 1, :], chunk)
        shifts[c] = chunk.astype(jnp.bfloat16)
    seen[...] = jnp.zeros(seen.shape, jnp.float32)
    mass[...] = jnp.zeros(mass.shape, jnp.float32)
    live = live_ref[0, 0]

    def scores(t, both):
        red, col = both & (TILE_BASE - 1), lax.shift_right_logical(both, TILE_BITS)
        if side == 0:
            red, col = col, red
        place = lane - (red & (PART - 1))
        ones = ((place == 0) | (place == PART) | (place == 2 * PART)).astype(jnp.float32).astype(jnp.bfloat16)
        ones = jnp.broadcast_to(ones, (3 * PART, BLOCK))
        lhs = red_ref[pl.ds(pl.multiple_of(red * BLOCK, BLOCK), BLOCK), :] + columns[red // PART]
        rhs = col_ref[:, pl.ds(pl.multiple_of(col * BLOCK, BLOCK), BLOCK)]
        rhs = jnp.concatenate([rhs, ones, shifts[col]], axis=0)
        score = jnp.dot(lhs, rhs, preferred_element_type=jnp.float32)
        return score.reshape(BLOCK // 8, 8, BLOCK), jnp.where(t < live, col, ncol)

    tiles = tiles_ref[...]

    own = [tiles[0, t] for t in range(tiles.shape[1])]

    def tile(t):
        score, slot = scores(t, own[t])
        terms = jnp.exp2(score * SCALE)
        mass[slot] = mass[slot] + jnp.sum(terms, axis=0)
        seen[pl.ds(slot, 1), :] = jnp.ones((1, LANES), jnp.float32)

    for t in range(tiles.shape[1]):
        tile(t)

    def finish(part):
        for h in (0, 1):
            rows[pl.ds(h, ncol, stride=2), :] = part[:, h * LANES : (h + 1) * LANES]
        copies, height, _ = out_ref.shape
        out_ref[:, : 2 * ncol, :] = jnp.broadcast_to(rows[...][None], (copies, 2 * ncol, LANES))
        if height > 2 * ncol:
            out_ref[:, 2 * ncol :, :] = jnp.broadcast_to(total_ref[...][None], (copies, height - 2 * ncol, LANES))

    total = jnp.sum(mass[:ncol], axis=1)
    good = (total > 1e-27) & (total < 1e30)
    finish(jnp.where(good, shift[...] + jnp.log2(jnp.where(good, total, 1.0)) * INV_SCALE, very_low))
    used = jnp.concatenate([seen[:ncol, :]] * 2, axis=1) > 0.0
    lost = jnp.max(jnp.where(used & real & jnp.logical_not(good), 1.0, 0.0))

    @pl.when(lost > 0.0)
    def _():
        fetch = pltpu.make_async_copy(tiles_ref, pairs_ref, sem)
        fetch.start()
        fetch.wait()
        peak[...] = jnp.full(peak.shape, very_low, jnp.float32)
        mass[...] = jnp.zeros(mass.shape, jnp.float32)

        def exact(t, _):
            score, slot = scores(t, pairs_ref[0, t])
            old = peak[slot]
            new = jnp.maximum(old, jnp.max(score, axis=0))
            terms = jnp.exp2((score - new[None]) * SCALE)
            mass[slot] = mass[slot] * jnp.exp2((old - new) * SCALE) + jnp.sum(terms, axis=0)
            peak[slot] = new
            return 0

        lax.fori_loop(0, live, exact, 0)
        tops = peak[:ncol]
        top = jnp.max(tops, axis=1, keepdims=True)
        total = jnp.sum(mass[:ncol] * jnp.exp2((tops - top) * SCALE), axis=1)
        some = total > 0.0
        finish(
            jnp.where(
                some, shift[...] + top.reshape(ncol, BLOCK) + jnp.log2(jnp.where(some, total, 1.0)) * INV_SCALE, very_low
            )
        )


def sweep(side, out, live, pairs, parts, red_real, last, col_real, total, red, col):
    nred, ncol = red.shape[0] // BLOCK, col.shape[1] // BLOCK
    return pl.pallas_call(
        functools.partial(sweep_kernel, side),
        out_shape=(
            jax.ShapeDtypeStruct(out, jnp.float32),
            jax.ShapeDtypeStruct((2 * nred, LANES), jnp.float32),
        ),
        in_specs=[SMEM] + [VMEM] * 8,
        out_specs=(VMEM, VMEM),
        scratch_shapes=[
            pltpu.VMEM((2 * ncol, LANES), jnp.float32),
            pltpu.VMEM((ncol, BLOCK), jnp.float32),
            pltpu.VMEM((ncol + 8, LANES), jnp.float32),
            pltpu.VMEM((ncol + 1, 8, BLOCK), jnp.float32),
            pltpu.VMEM((ncol + 1, 8, BLOCK), jnp.float32),
            pltpu.VMEM((nred // PART, BLOCK, LANES), jnp.bfloat16),
            pltpu.VMEM((ncol, PART, BLOCK), jnp.bfloat16),
            pltpu.SMEM(pairs.shape, jnp.int32),
            pltpu.SemaphoreType.DMA,
        ],
        compiler_params=PARAMS,
    )(live, pairs, parts, red_real, last, col_real, total, red, col)


def relay_kernel(rows, first, parts_ref, out_ref):
    copies, height, _ = out_ref.shape
    start = 0
    if first:
        start = pl.multiple_of(lax.axis_index("core") * rows, rows)
    value = merged(parts_ref[:, pl.ds(start, rows), :])
    out_ref[:, :rows, :] = jnp.broadcast_to(value[None], (copies, rows, LANES))
    extra = height - rows
    if extra:
        count = jnp.sum(parts_ref[:, parts_ref.shape[1] - extra :, :], axis=0)
        out_ref[:, rows:, :] = jnp.broadcast_to(count[None], (copies, extra, LANES))


def relay(rows, extra, copies, first, parts):
    return pl.pallas_call(
        functools.partial(relay_kernel, rows, first),
        out_shape=jax.ShapeDtypeStruct((copies, rows + extra, LANES), jnp.float32),
        in_specs=[VMEM],
        out_specs=VMEM,
        compiler_params=PARAMS,
    )(parts)


def finish_kernel(
    src_value, src_half, src_real, tgt_parts, tgt_half, tgt_real, first_src, first_tgt, src_out, tgt_out
):
    half = tgt_half.shape[0] // 2
    log_tgt = jnp.log(jnp.sum(first_src[:, src_half.shape[0] :, :], axis=0)[:1])
    log_src = jnp.log(sum(first_tgt[i, half:, :] for i in range(0, first_tgt.shape[0], 2))[:1])
    src_shift = -epsilon * (ITERS * log_src - (ITERS - 1) * log_tgt)
    tgt_shift = epsilon * ITERS * (log_src - log_tgt)
    for half, value, shift, real, out in (
        (src_half, src_value[...], src_shift, src_real, src_out),
        (tgt_half, whole(tgt_parts, tgt_half.shape[0]), tgt_shift, tgt_real, tgt_out),
    ):
        out[...] = jnp.where(real[...] > 0.0, (half[...] - value) * (2.0 / DIM) + shift, 0.0)


def finish(src_value, src_half, src_real, tgt_parts, tgt_half, tgt_real, first_src, first_tgt):
    return pl.pallas_call(
        finish_kernel,
        out_shape=(
            jax.ShapeDtypeStruct(src_half.shape, jnp.float32),
            jax.ShapeDtypeStruct(tgt_half.shape, jnp.float32),
        ),
        in_specs=[VMEM] * 8,
        out_specs=(VMEM, VMEM),
        compiler_params=PARAMS,
    )(src_value, src_half, src_real, tgt_parts, tgt_half, tgt_real, first_src, first_tgt)


def on_device(sizes, src_points, tgt_points, src_counts, tgt_counts, tile_list, tile_count):
    pairs = tile_list.reshape(tile_list.shape[2:]).T
    src, tgt, src_half, tgt_half, src_real, tgt_real, src_total, tgt_total, pairs, src_t, tgt_t = prepare(
        src_counts, tgt_counts, src_points.T, tgt_points.T, pairs
    )
    src_rows = src_half.shape[0]
    tgt_rows = tgt_half.shape[0]

    tgt_parts = tgt_half
    src_value = src_half
    first = []
    for step in range(ITERS):
        extra = src_total.shape[0] if step == 0 else 0
        out = (sizes["y"], src_rows + extra, LANES)
        src_parts, tgt_value = sweep(
            1, out, tile_count, pairs, tgt_parts, tgt_real, src_value, src_real, tgt_total, tgt, src_t
        )
        src_parts = lax.all_to_all(src_parts, "y", 0, 0)
        out = (1, tgt_rows + extra, LANES)
        tgt_parts, src_value = sweep(
            0, out, tile_count, pairs, src_parts, src_real, tgt_value, tgt_real, src_total, src, tgt_t
        )
        tgt_parts = lax.all_gather(tgt_parts, "core", axis=0, tiled=True)
        tgt_parts = relay(tgt_rows // 2, extra, sizes["z"], True, tgt_parts)
        tgt_parts = lax.all_to_all(tgt_parts, "z", 0, 0)
        tgt_parts = relay(tgt_rows // 2, extra, sizes["x"] * sizes["core"], False, tgt_parts)
        tgt_parts = lax.all_to_all(tgt_parts, ("x", "core"), 0, 0)
        if step == 0:
            first = [src_parts, tgt_parts]
    src_out, tgt_out = finish(src_value, src_half, src_real, tgt_parts, tgt_half, tgt_real, *first)
    return (src_out.reshape(-1), tgt_out.reshape(-1))


def solution(mesh):
    sizes = {"x": 4, "z": 8, "core": 2, "y": mesh.shape["col"]}
    fine = Mesh(mesh.devices.reshape(tuple(sizes.values())), tuple(sizes))
    row = ("x", "z", "core")
    return jax.shard_map(
        functools.partial(on_device, sizes),
        mesh=fine,
        in_specs=(P(row, None), P("y", None), P(row), P("y"), P(row, "y", None, None), P(row, "y")),
        out_specs=(P(row), P("y")),
        check_vma=False,
    )
```

```python
import functools
import math

import jax
import jax.numpy as jnp
from jax import lax
from jax.experimental import pallas as pl
from jax.experimental.pallas import tpu as pltpu
from jax.sharding import Mesh, PartitionSpec as P

BLOCK = 256
ITERS = 3
LANES = 128
PART_BITS = 4
PART = 1 << PART_BITS
TILE_BITS = 8
TILE_BASE = 1 << TILE_BITS

epsilon = 0.05
very_low = -1e30
DIM = 64
SCALE = 2.0 / (DIM * epsilon) * math.log2(math.e)
INV_SCALE = 1.0 / SCALE

SMEM = pl.BlockSpec(memory_space=pltpu.SMEM)
HBM = pl.BlockSpec(memory_space=pltpu.HBM)
VMEM = pl.BlockSpec(memory_space=pltpu.VMEM)
PARAMS = pltpu.CompilerParams(vmem_limit_bytes=24 * 1024 * 1024)


def in_hbm(*arrays):
    return [pltpu.with_memory_space_constraint(a, pltpu.HBM) for a in arrays]


def merged(parts):
    top = jnp.max(parts, axis=0)
    total = jnp.sum(jnp.exp2((parts - top[None]) * SCALE), axis=0)
    return top + jnp.log2(total) * INV_SCALE


def prepare_kernel(live_ref, counts_s, counts_t, src_t, tgt_t, pairs_in, src, tgt, half_s, half_t, real_s, real_t, sum_s, sum_t, must, tiles, hot, xs, xt, cs, ct, pairs, sems):
    copies = [
        pltpu.make_async_copy(a, b, sems.at[i])
        for i, (a, b) in enumerate(((counts_s, cs), (src_t, xs), (counts_t, ct), (tgt_t, xt), (pairs_in, pairs)))
    ]
    for copy in copies:
        copy.start()
    row = lax.broadcasted_iota(jnp.int32, (3 * PART, BLOCK), 0) & (PART - 1)
    for block in range(PART):
        hot[block] = (row == block).astype(jnp.float32).astype(jnp.bfloat16)
    lane = lax.broadcasted_iota(jnp.int32, (1, LANES), 1)
    for side, (counts, points, out, norms, real, total) in enumerate(
        ((cs, xs, src, half_s, real_s, sum_s), (ct, xt, tgt, half_t, real_t, sum_t))
    ):
        copies[2 * side].wait()
        copies[2 * side + 1].wait()
        count = sum(counts[i] for i in range(counts.shape[0]))
        total[...] = jnp.full(total.shape, count).astype(jnp.float32)
        for row in range(norms.shape[0]):
            chunk = points[:, row * LANES : (row + 1) * LANES].astype(jnp.float32)
            norms[row : row + 1, :] = 0.5 * jnp.sum(chunk * chunk, axis=0, keepdims=True)
            chunk = jnp.concatenate([chunk, jnp.zeros((LANES - DIM, LANES), jnp.float32)], axis=0)
            out[row * LANES : (row + 1) * LANES, :] = chunk.T.astype(jnp.bfloat16)
            slot = lane + (row % 2) * LANES
            real[row : row + 1, :] = (slot < counts[row // 2]).astype(jnp.float32)
    copies[4].wait()
    tiles[...] = pairs[:1, :] * TILE_BASE + pairs[1:, :]
    blocks = real_t.shape[0] // 2
    shape = (blocks, pairs.shape[1])
    own = pairs[1:, :] == lax.broadcasted_iota(jnp.int32, shape, 0)
    own = own & (lax.broadcasted_iota(jnp.int32, shape, 1) < live_ref[0, 0])
    used = jnp.max(jnp.where(own, 1.0, 0.0), axis=1, keepdims=True)
    for h in (0, 1):
        half = pl.ds(h, blocks, stride=2)
        must[half, :] = real_t[half, :] * used


def prepare(live, src_counts, tgt_counts, src_t, tgt_t, pairs):
    ns, nt = src_t.shape[1], tgt_t.shape[1]
    rows_s = jax.ShapeDtypeStruct((ns // LANES, LANES), jnp.float32)
    rows_t = jax.ShapeDtypeStruct((nt // LANES, LANES), jnp.float32)
    total = jax.ShapeDtypeStruct((8, LANES), jnp.float32)
    return pl.pallas_call(
        prepare_kernel,
        out_shape=(
            jax.ShapeDtypeStruct((ns, LANES), jnp.bfloat16),
            jax.ShapeDtypeStruct((nt, LANES), jnp.bfloat16),
            rows_s,
            rows_t,
            rows_s,
            rows_t,
            total,
            total,
            rows_t,
            jax.ShapeDtypeStruct((1, pairs.shape[1]), jnp.int32),
            jax.ShapeDtypeStruct((PART, 3 * PART, BLOCK), jnp.bfloat16),
            jax.ShapeDtypeStruct(src_t.shape, jnp.bfloat16),
            jax.ShapeDtypeStruct(tgt_t.shape, jnp.bfloat16),
        ),
        in_specs=[SMEM] + [HBM] * 5,
        out_specs=(VMEM,) * 13,
        scratch_shapes=[
            pltpu.SMEM(src_counts.shape, jnp.int32),
            pltpu.SMEM(tgt_counts.shape, jnp.int32),
            pltpu.VMEM(pairs.shape, jnp.int32),
            pltpu.SemaphoreType.DMA((5,)),
        ],
        compiler_params=PARAMS,
    )(live, *in_hbm(src_counts, tgt_counts, src_t, tgt_t, pairs))


def whole(parts_ref, rows):
    count, height, _ = parts_ref.shape
    if height >= rows:
        return merged(parts_ref[:, :rows, :])
    half = rows // 2
    return jnp.concatenate(
        [merged(jnp.stack([parts_ref[i, :half, :] for i in range(c, count, 2)])) for c in (0, 1)], axis=0
    )


def split(value):
    hi = value.astype(jnp.bfloat16).astype(jnp.float32)
    rest = value - hi
    mid = rest.astype(jnp.bfloat16).astype(jnp.float32)
    return hi, mid, rest - mid


def by_block(rows_ref):
    blocks = rows_ref.shape[0] // 2
    return jnp.concatenate([rows_ref[pl.ds(h, blocks, stride=2), :] for h in (0, 1)], axis=1)


def sweep_kernel(
    side, live_ref, tiles_ref, hot_ref, parts_ref, red_real, last_ref, col_real, col_must, total_ref, red_ref, col_ref,
    out_ref, value_ref, rows, shift, peak, mass, columns, shifts, pairs_ref, sem,
):
    nred = red_ref.shape[0] // BLOCK
    ncol = col_ref.shape[1] // BLOCK
    value_ref[...] = whole(parts_ref, 2 * nred) if len(parts_ref.shape) == 3 else parts_ref[...]
    bias = jnp.where(by_block(red_real) > 0.0, -by_block(value_ref), very_low)
    hi, mid, low = split(bias)
    for i in range(nred // PART):
        own = slice(i * PART, (i + 1) * PART)
        ones = (lax.broadcasted_iota(jnp.int32, (PART, BLOCK), 0) < 3).astype(jnp.float32)
        pieces = [jnp.zeros((DIM, BLOCK), jnp.float32), hi[own], mid[own], low[own], ones]
        columns[i] = jnp.concatenate(pieces, axis=0).T.astype(jnp.bfloat16)
    real = by_block(col_real) > 0.0
    last = jnp.where(real, by_block(last_ref), 0.0)
    shift[...] = last
    lower = split(-last)
    row = lax.broadcasted_iota(jnp.int32, (PART, BLOCK), 0)
    for c in range(ncol):
        chunk = jnp.zeros((PART, BLOCK), jnp.float32)
        for i in range(3):
            chunk = jnp.where(row == i, lower[i][c : c + 1, :], chunk)
        shifts[c] = chunk.astype(jnp.bfloat16)
    mass[...] = jnp.zeros(mass.shape, jnp.float32)
    live = live_ref[0, 0]

    def scores(t, both):
        red, col = both & (TILE_BASE - 1), lax.shift_right_logical(both, TILE_BITS)
        if side == 0:
            red, col = col, red
        lhs = red_ref[pl.ds(pl.multiple_of(red * BLOCK, BLOCK), BLOCK), :] + columns[lax.shift_right_logical(red, PART_BITS)]
        rhs = col_ref[:, pl.ds(pl.multiple_of(col * BLOCK, BLOCK), BLOCK)]
        rhs = jnp.concatenate([rhs, hot_ref[red & (PART - 1)], shifts[col]], axis=0)
        score = jnp.dot(lhs, rhs, preferred_element_type=jnp.float32)
        return score.reshape(BLOCK // 8, 8, BLOCK), jnp.where(t < live, col, ncol)

    tiles = tiles_ref[...]

    own = [tiles[0, t] for t in range(tiles.shape[1])]

    def tile(t):
        score, slot = scores(t, own[t])
        terms = jnp.exp2(score * SCALE)
        mass[slot] = mass[slot] + jnp.sum(terms, axis=0)

    for t in range(tiles.shape[1]):
        tile(t)

    def finish(part):
        for h in (0, 1):
            rows[pl.ds(h, ncol, stride=2), :] = part[:, h * LANES : (h + 1) * LANES]
        copies, height, _ = out_ref.shape
        out_ref[:, : 2 * ncol, :] = jnp.broadcast_to(rows[...][None], (copies, 2 * ncol, LANES))
        if height > 2 * ncol:
            out_ref[:, 2 * ncol :, :] = jnp.broadcast_to(total_ref[...][None], (copies, height - 2 * ncol, LANES))

    total = jnp.sum(mass[:ncol], axis=1)
    good = (total > 1e-27) & (total < 1e30)
    finish(jnp.where(good, shift[...] + jnp.log2(jnp.where(good, total, 1.0)) * INV_SCALE, very_low))
    lost = jnp.max(jnp.where(good, 0.0, by_block(col_must)))

    @pl.when(lost > 0.0)
    def _():
        fetch = pltpu.make_async_copy(tiles_ref, pairs_ref, sem)
        fetch.start()
        fetch.wait()
        peak[...] = jnp.full(peak.shape, very_low, jnp.float32)
        mass[...] = jnp.zeros(mass.shape, jnp.float32)

        def exact(t, _):
            score, slot = scores(t, pairs_ref[0, t])
            old = peak[slot]
            new = jnp.maximum(old, jnp.max(score, axis=0))
            terms = jnp.exp2((score - new[None]) * SCALE)
            mass[slot] = mass[slot] * jnp.exp2((old - new) * SCALE) + jnp.sum(terms, axis=0)
            peak[slot] = new
            return 0

        lax.fori_loop(0, live, exact, 0)
        tops = peak[:ncol]
        top = jnp.max(tops, axis=1, keepdims=True)
        total = jnp.sum(mass[:ncol] * jnp.exp2((tops - top) * SCALE), axis=1)
        some = total > 0.0
        finish(
            jnp.where(
                some, shift[...] + top.reshape(ncol, BLOCK) + jnp.log2(jnp.where(some, total, 1.0)) * INV_SCALE, very_low
            )
        )


def sweep(side, out, live, tiles, hot, parts, red_real, last, col_real, col_must, total, red, col):
    nred, ncol = red.shape[0] // BLOCK, col.shape[1] // BLOCK
    return pl.pallas_call(
        functools.partial(sweep_kernel, side),
        out_shape=(
            jax.ShapeDtypeStruct(out, jnp.float32),
            jax.ShapeDtypeStruct((2 * nred, LANES), jnp.float32),
        ),
        in_specs=[SMEM] + [VMEM] * 10,
        out_specs=(VMEM, VMEM),
        scratch_shapes=[
            pltpu.VMEM((2 * ncol, LANES), jnp.float32),
            pltpu.VMEM((ncol, BLOCK), jnp.float32),
            pltpu.VMEM((ncol + 1, 8, BLOCK), jnp.float32),
            pltpu.VMEM((ncol + 1, 8, BLOCK), jnp.float32),
            pltpu.VMEM((nred // PART, BLOCK, LANES), jnp.bfloat16),
            pltpu.VMEM((ncol, PART, BLOCK), jnp.bfloat16),
            pltpu.SMEM(tiles.shape, jnp.int32),
            pltpu.SemaphoreType.DMA,
        ],
        compiler_params=PARAMS,
    )(live, tiles, hot, parts, red_real, last, col_real, col_must, total, red, col)


def relay_kernel(rows, first, parts_ref, out_ref):
    copies, height, _ = out_ref.shape
    start = 0
    if first:
        start = pl.multiple_of(lax.axis_index("core") * rows, rows)
    value = merged(parts_ref[:, pl.ds(start, rows), :])
    out_ref[:, :rows, :] = jnp.broadcast_to(value[None], (copies, rows, LANES))
    extra = height - rows
    if extra:
        count = jnp.sum(parts_ref[:, parts_ref.shape[1] - extra :, :], axis=0)
        out_ref[:, rows:, :] = jnp.broadcast_to(count[None], (copies, extra, LANES))


def relay(rows, extra, copies, first, parts):
    return pl.pallas_call(
        functools.partial(relay_kernel, rows, first),
        out_shape=jax.ShapeDtypeStruct((copies, rows + extra, LANES), jnp.float32),
        in_specs=[VMEM],
        out_specs=VMEM,
        compiler_params=PARAMS,
    )(parts)


def finish_kernel(
    src_value, src_half, src_real, tgt_parts, tgt_half, tgt_real, first_src, first_tgt, src_out, tgt_out
):
    half = tgt_half.shape[0] // 2
    log_tgt = jnp.log(jnp.sum(first_src[:, src_half.shape[0] :, :], axis=0)[:1])
    log_src = jnp.log(sum(first_tgt[i, half:, :] for i in range(0, first_tgt.shape[0], 2))[:1])
    src_shift = -epsilon * (ITERS * log_src - (ITERS - 1) * log_tgt)
    tgt_shift = epsilon * ITERS * (log_src - log_tgt)
    for half, value, shift, real, out in (
        (src_half, src_value[...], src_shift, src_real, src_out),
        (tgt_half, whole(tgt_parts, tgt_half.shape[0]), tgt_shift, tgt_real, tgt_out),
    ):
        out[...] = jnp.where(real[...] > 0.0, (half[...] - value) * (2.0 / DIM) + shift, 0.0)


def finish(src_value, src_half, src_real, tgt_parts, tgt_half, tgt_real, first_src, first_tgt):
    return pl.pallas_call(
        finish_kernel,
        out_shape=(
            jax.ShapeDtypeStruct(src_half.shape, jnp.float32),
            jax.ShapeDtypeStruct(tgt_half.shape, jnp.float32),
        ),
        in_specs=[VMEM] * 8,
        out_specs=(VMEM, VMEM),
        compiler_params=PARAMS,
    )(src_value, src_half, src_real, tgt_parts, tgt_half, tgt_real, first_src, first_tgt)


def on_device(sizes, src_points, tgt_points, src_counts, tgt_counts, tile_list, tile_count):
    pairs = tile_list.reshape(tile_list.shape[2:]).T
    src, tgt, src_half, tgt_half, src_real, tgt_real, src_total, tgt_total, must, tiles, hot, src_t, tgt_t = prepare(
        tile_count, src_counts, tgt_counts, src_points.T, tgt_points.T, pairs
    )
    src_rows = src_half.shape[0]
    tgt_rows = tgt_half.shape[0]

    tgt_parts = tgt_half
    src_value = src_half
    first = []
    for step in range(ITERS):
        extra = src_total.shape[0] if step == 0 else 0
        out = (sizes["y"], src_rows + extra, LANES)
        src_parts, tgt_value = sweep(
            1, out, tile_count, tiles, hot, tgt_parts, tgt_real, src_value, src_real, src_real, tgt_total, tgt, src_t
        )
        src_parts = lax.all_to_all(src_parts, "y", 0, 0)
        out = (1, tgt_rows + extra, LANES)
        tgt_parts, src_value = sweep(
            0, out, tile_count, tiles, hot, src_parts, src_real, tgt_value, tgt_real, must, src_total, src, tgt_t
        )
        tgt_parts = lax.all_gather(tgt_parts, "core", axis=0, tiled=True)
        tgt_parts = relay(tgt_rows // 2, extra, sizes["z"], True, tgt_parts)
        tgt_parts = lax.all_to_all(tgt_parts, "z", 0, 0)
        tgt_parts = relay(tgt_rows // 2, extra, sizes["x"] * sizes["core"], False, tgt_parts)
        tgt_parts = lax.all_to_all(tgt_parts, ("x", "core"), 0, 0)
        if step == 0:
            first = [src_parts, tgt_parts]
    src_out, tgt_out = finish(src_value, src_half, src_real, tgt_parts, tgt_half, tgt_real, *first)
    return (src_out.reshape(-1), tgt_out.reshape(-1))


def solution(mesh):
    sizes = {"x": 4, "z": 8, "core": 2, "y": mesh.shape["col"]}
    fine = Mesh(mesh.devices.reshape(tuple(sizes.values())), tuple(sizes))
    row = ("x", "z", "core")
    return jax.shard_map(
        functools.partial(on_device, sizes),
        mesh=fine,
        in_specs=(P(row, None), P("y", None), P(row), P("y"), P(row, "y", None, None), P(row, "y")),
        out_specs=(P(row), P("y")),
        check_vma=False,
    )
```

```python
import functools
import math

import jax
import jax.numpy as jnp
from jax import lax
from jax.experimental import pallas as pl
from jax.experimental.pallas import tpu as pltpu
from jax.sharding import Mesh, PartitionSpec as P

BLOCK = 256
ITERS = 3
LANES = 128
PART_BITS = 4
PART = 1 << PART_BITS
TILE_BITS = 8
TILE_BASE = 1 << TILE_BITS

epsilon = 0.05
very_low = -1e30
DIM = 64
SCALE = 2.0 / (DIM * epsilon) * math.log2(math.e)
INV_SCALE = 1.0 / SCALE

SMEM = pl.BlockSpec(memory_space=pltpu.SMEM)
HBM = pl.BlockSpec(memory_space=pltpu.HBM)
VMEM = pl.BlockSpec(memory_space=pltpu.VMEM)
PARAMS = pltpu.CompilerParams(vmem_limit_bytes=24 * 1024 * 1024)


def in_hbm(*arrays):
    return [pltpu.with_memory_space_constraint(a, pltpu.HBM) for a in arrays]


def merged(parts):
    top = jnp.max(parts, axis=0)
    total = jnp.sum(jnp.exp2((parts - top[None]) * SCALE), axis=0)
    return top + jnp.log2(total) * INV_SCALE


def prepare_kernel(live_ref, counts_s, counts_t, src_t, tgt_t, pairs_in, src, tgt, half_s, half_t, real_s, real_t, sum_s, sum_t, must, tiles, hot, xs, xt, cs, ct, pairs, sems):
    copies = [
        pltpu.make_async_copy(a, b, sems.at[i])
        for i, (a, b) in enumerate(((counts_s, cs), (src_t, xs), (counts_t, ct), (tgt_t, xt), (pairs_in, pairs)))
    ]
    for copy in copies:
        copy.start()
    row = lax.broadcasted_iota(jnp.int32, (3 * PART, BLOCK), 0) & (PART - 1)
    for block in range(PART):
        hot[block] = (row == block).astype(jnp.float32).astype(jnp.bfloat16)
    lane = lax.broadcasted_iota(jnp.int32, (1, LANES), 1)
    for side, (counts, points, out, norms, real, total) in enumerate(
        ((cs, xs, src, half_s, real_s, sum_s), (ct, xt, tgt, half_t, real_t, sum_t))
    ):
        copies[2 * side].wait()
        copies[2 * side + 1].wait()
        count = sum(counts[i] for i in range(counts.shape[0]))
        total[...] = jnp.full(total.shape, count).astype(jnp.float32)
        for row in range(norms.shape[0]):
            chunk = points[:, row * LANES : (row + 1) * LANES].astype(jnp.float32)
            norms[row : row + 1, :] = 0.5 * jnp.sum(chunk * chunk, axis=0, keepdims=True)
            chunk = jnp.concatenate([chunk, jnp.zeros((LANES - DIM, LANES), jnp.float32)], axis=0)
            out[row * LANES : (row + 1) * LANES, :] = chunk.T.astype(jnp.bfloat16)
            slot = lane + (row % 2) * LANES
            real[row : row + 1, :] = (slot < counts[row // 2]).astype(jnp.float32)
    copies[4].wait()
    tiles[...] = pairs[:1, :] * TILE_BASE + pairs[1:, :]
    blocks = real_t.shape[0] // 2
    shape = (blocks, pairs.shape[1])
    own = pairs[1:, :] == lax.broadcasted_iota(jnp.int32, shape, 0)
    own = own & (lax.broadcasted_iota(jnp.int32, shape, 1) < live_ref[0, 0])
    used = jnp.max(jnp.where(own, 1.0, 0.0), axis=1, keepdims=True)
    for h in (0, 1):
        half = pl.ds(h, blocks, stride=2)
        must[half, :] = real_t[half, :] * used


def prepare(live, src_counts, tgt_counts, src_t, tgt_t, pairs):
    ns, nt = src_t.shape[1], tgt_t.shape[1]
    rows_s = jax.ShapeDtypeStruct((ns // LANES, LANES), jnp.float32)
    rows_t = jax.ShapeDtypeStruct((nt // LANES, LANES), jnp.float32)
    total = jax.ShapeDtypeStruct((8, LANES), jnp.float32)
    return pl.pallas_call(
        prepare_kernel,
        out_shape=(
            jax.ShapeDtypeStruct((ns, LANES), jnp.bfloat16),
            jax.ShapeDtypeStruct((nt, LANES), jnp.bfloat16),
            rows_s,
            rows_t,
            rows_s,
            rows_t,
            total,
            total,
            rows_t,
            jax.ShapeDtypeStruct((1, pairs.shape[1]), jnp.int32),
            jax.ShapeDtypeStruct((PART, 3 * PART, BLOCK), jnp.bfloat16),
            jax.ShapeDtypeStruct(src_t.shape, jnp.bfloat16),
            jax.ShapeDtypeStruct(tgt_t.shape, jnp.bfloat16),
        ),
        in_specs=[SMEM] + [HBM] * 5,
        out_specs=(VMEM,) * 13,
        scratch_shapes=[
            pltpu.SMEM(src_counts.shape, jnp.int32),
            pltpu.SMEM(tgt_counts.shape, jnp.int32),
            pltpu.VMEM(pairs.shape, jnp.int32),
            pltpu.SemaphoreType.DMA((5,)),
        ],
        compiler_params=PARAMS,
    )(live, *in_hbm(src_counts, tgt_counts, src_t, tgt_t, pairs))


def whole(parts_ref, rows):
    count, height, _ = parts_ref.shape
    if height >= rows:
        return merged(parts_ref[:, :rows, :])
    return jnp.concatenate([parts_ref[c, : rows // 2, :] for c in range(count)], axis=0)


def split(value):
    hi = value.astype(jnp.bfloat16).astype(jnp.float32)
    rest = value - hi
    mid = rest.astype(jnp.bfloat16).astype(jnp.float32)
    return hi, mid, rest - mid


def by_block(rows_ref):
    blocks = rows_ref.shape[0] // 2
    return jnp.concatenate([rows_ref[pl.ds(h, blocks, stride=2), :] for h in (0, 1)], axis=1)


def sweep_kernel(
    side, live_ref, tiles_ref, hot_ref, parts_ref, red_real, last_ref, col_real, col_must, total_ref, red_ref, col_ref,
    out_ref, value_ref, rows, shift, peak, mass, columns, shifts, pairs_ref, sem,
):
    nred = red_ref.shape[0] // BLOCK
    ncol = col_ref.shape[1] // BLOCK
    value_ref[...] = whole(parts_ref, 2 * nred) if len(parts_ref.shape) == 3 else parts_ref[...]
    bias = jnp.where(by_block(red_real) > 0.0, -by_block(value_ref), very_low)
    hi, mid, low = split(bias)
    for i in range(nred // PART):
        own = slice(i * PART, (i + 1) * PART)
        ones = (lax.broadcasted_iota(jnp.int32, (PART, BLOCK), 0) < 3).astype(jnp.float32)
        pieces = [jnp.zeros((DIM, BLOCK), jnp.float32), hi[own], mid[own], low[own], ones]
        columns[i] = jnp.concatenate(pieces, axis=0).T.astype(jnp.bfloat16)
    real = by_block(col_real) > 0.0
    last = jnp.where(real, by_block(last_ref), 0.0)
    shift[...] = last
    lower = split(-last)
    row = lax.broadcasted_iota(jnp.int32, (PART, BLOCK), 0)
    for c in range(ncol):
        chunk = jnp.zeros((PART, BLOCK), jnp.float32)
        for i in range(3):
            chunk = jnp.where(row == i, lower[i][c : c + 1, :], chunk)
        shifts[c] = chunk.astype(jnp.bfloat16)
    mass[...] = jnp.zeros(mass.shape, jnp.float32)
    live = live_ref[0, 0]

    def scores(t, both):
        red, col = both & (TILE_BASE - 1), lax.shift_right_logical(both, TILE_BITS)
        if side == 0:
            red, col = col, red
        lhs = red_ref[pl.ds(pl.multiple_of(red * BLOCK, BLOCK), BLOCK), :] + columns[lax.shift_right_logical(red, PART_BITS)]
        rhs = col_ref[:, pl.ds(pl.multiple_of(col * BLOCK, BLOCK), BLOCK)]
        rhs = jnp.concatenate([rhs, hot_ref[red & (PART - 1)], shifts[col]], axis=0)
        score = jnp.dot(lhs, rhs, preferred_element_type=jnp.float32)
        return score.reshape(BLOCK // 8, 8, BLOCK), jnp.where(t < live, col, ncol)

    tiles = tiles_ref[...]

    own = [tiles[0, t] for t in range(tiles.shape[1])]

    def tile(t):
        score, slot = scores(t, own[t])
        terms = jnp.exp2(score * SCALE)
        mass[slot] = mass[slot] + jnp.sum(terms, axis=0)

    for t in range(tiles.shape[1]):
        tile(t)

    def finish(part):
        for h in (0, 1):
            rows[pl.ds(h, ncol, stride=2), :] = part[:, h * LANES : (h + 1) * LANES]
        copies, height, _ = out_ref.shape
        share = 2 * ncol if side == 1 else ncol
        for i in range(copies):
            start = 0 if side == 1 else i % 2 * share
            out_ref[i, :share, :] = rows[start : start + share, :]
            if height > share:
                out_ref[i, share:, :] = total_ref[...]

    total = jnp.sum(mass[:ncol], axis=1)
    good = (total > 1e-27) & (total < 1e30)
    finish(jnp.where(good, shift[...] + jnp.log2(jnp.where(good, total, 1.0)) * INV_SCALE, very_low))
    lost = jnp.max(jnp.where(good, 0.0, by_block(col_must)))

    @pl.when(lost > 0.0)
    def _():
        fetch = pltpu.make_async_copy(tiles_ref, pairs_ref, sem)
        fetch.start()
        fetch.wait()
        peak[...] = jnp.full(peak.shape, very_low, jnp.float32)
        mass[...] = jnp.zeros(mass.shape, jnp.float32)

        def exact(t, _):
            score, slot = scores(t, pairs_ref[0, t])
            old = peak[slot]
            new = jnp.maximum(old, jnp.max(score, axis=0))
            terms = jnp.exp2((score - new[None]) * SCALE)
            mass[slot] = mass[slot] * jnp.exp2((old - new) * SCALE) + jnp.sum(terms, axis=0)
            peak[slot] = new
            return 0

        lax.fori_loop(0, live, exact, 0)
        tops = peak[:ncol]
        top = jnp.max(tops, axis=1, keepdims=True)
        total = jnp.sum(mass[:ncol] * jnp.exp2((tops - top) * SCALE), axis=1)
        some = total > 0.0
        finish(
            jnp.where(
                some, shift[...] + top.reshape(ncol, BLOCK) + jnp.log2(jnp.where(some, total, 1.0)) * INV_SCALE, very_low
            )
        )


def sweep(side, out, live, tiles, hot, parts, red_real, last, col_real, col_must, total, red, col):
    nred, ncol = red.shape[0] // BLOCK, col.shape[1] // BLOCK
    return pl.pallas_call(
        functools.partial(sweep_kernel, side),
        out_shape=(
            jax.ShapeDtypeStruct(out, jnp.float32),
            jax.ShapeDtypeStruct((2 * nred, LANES), jnp.float32),
        ),
        in_specs=[SMEM] + [VMEM] * 10,
        out_specs=(VMEM, VMEM),
        scratch_shapes=[
            pltpu.VMEM((2 * ncol, LANES), jnp.float32),
            pltpu.VMEM((ncol, BLOCK), jnp.float32),
            pltpu.VMEM((ncol + 1, 8, BLOCK), jnp.float32),
            pltpu.VMEM((ncol + 1, 8, BLOCK), jnp.float32),
            pltpu.VMEM((nred // PART, BLOCK, LANES), jnp.bfloat16),
            pltpu.VMEM((ncol, PART, BLOCK), jnp.bfloat16),
            pltpu.SMEM(tiles.shape, jnp.int32),
            pltpu.SemaphoreType.DMA,
        ],
        compiler_params=PARAMS,
    )(live, tiles, hot, parts, red_real, last, col_real, col_must, total, red, col)


def relay_kernel(rows, parts_ref, out_ref):
    copies, height, _ = out_ref.shape
    value = merged(parts_ref[:, :rows, :])
    out_ref[:, :rows, :] = jnp.broadcast_to(value[None], (copies, rows, LANES))
    extra = height - rows
    if extra:
        count = jnp.sum(parts_ref[:, parts_ref.shape[1] - extra :, :], axis=0)
        out_ref[:, rows:, :] = jnp.broadcast_to(count[None], (copies, extra, LANES))


def relay(rows, extra, copies, parts):
    return pl.pallas_call(
        functools.partial(relay_kernel, rows),
        out_shape=jax.ShapeDtypeStruct((copies, rows + extra, LANES), jnp.float32),
        in_specs=[VMEM],
        out_specs=VMEM,
        compiler_params=PARAMS,
    )(parts)


def finish_kernel(
    src_value, src_half, src_real, tgt_parts, tgt_half, tgt_real, first_src, first_tgt, src_out, tgt_out
):
    half = tgt_half.shape[0] // 2
    log_tgt = jnp.log(jnp.sum(first_src[:, src_half.shape[0] :, :], axis=0)[:1])
    log_src = jnp.log(first_tgt[0, half : half + 1, :])
    src_shift = -epsilon * (ITERS * log_src - (ITERS - 1) * log_tgt)
    tgt_shift = epsilon * ITERS * (log_src - log_tgt)
    for half, value, shift, real, out in (
        (src_half, src_value[...], src_shift, src_real, src_out),
        (tgt_half, whole(tgt_parts, tgt_half.shape[0]), tgt_shift, tgt_real, tgt_out),
    ):
        out[...] = jnp.where(real[...] > 0.0, (half[...] - value) * (2.0 / DIM) + shift, 0.0)


def finish(src_value, src_half, src_real, tgt_parts, tgt_half, tgt_real, first_src, first_tgt):
    return pl.pallas_call(
        finish_kernel,
        out_shape=(
            jax.ShapeDtypeStruct(src_half.shape, jnp.float32),
            jax.ShapeDtypeStruct(tgt_half.shape, jnp.float32),
        ),
        in_specs=[VMEM] * 8,
        out_specs=(VMEM, VMEM),
        compiler_params=PARAMS,
    )(src_value, src_half, src_real, tgt_parts, tgt_half, tgt_real, first_src, first_tgt)


def on_device(sizes, src_points, tgt_points, src_counts, tgt_counts, tile_list, tile_count):
    pairs = tile_list.reshape(tile_list.shape[2:]).T
    src, tgt, src_half, tgt_half, src_real, tgt_real, src_total, tgt_total, must, tiles, hot, src_t, tgt_t = prepare(
        tile_count, src_counts, tgt_counts, src_points.T, tgt_points.T, pairs
    )
    src_rows = src_half.shape[0]
    tgt_rows = tgt_half.shape[0]

    tgt_parts = tgt_half
    src_value = src_half
    first = []
    for step in range(ITERS):
        extra = src_total.shape[0] if step == 0 else 0
        out = (sizes["y"], src_rows + extra, LANES)
        src_parts, tgt_value = sweep(
            1, out, tile_count, tiles, hot, tgt_parts, tgt_real, src_value, src_real, src_real, tgt_total, tgt, src_t
        )
        src_parts = lax.all_to_all(src_parts, "y", 0, 0)
        out = (sizes["x"] * sizes["core"], tgt_rows // 2 + extra, LANES)
        tgt_parts, src_value = sweep(
            0, out, tile_count, tiles, hot, src_parts, src_real, tgt_value, tgt_real, must, src_total, src, tgt_t
        )
        tgt_parts = lax.all_to_all(tgt_parts, ("x", "core"), 0, 0)
        tgt_parts = relay(tgt_rows // 2, extra, sizes["z"], tgt_parts)
        tgt_parts = lax.all_to_all(tgt_parts, "z", 0, 0)
        tgt_parts = relay(tgt_rows // 2, extra, 1, tgt_parts)
        tgt_parts = lax.all_gather(tgt_parts, "core", axis=0, tiled=True)
        if step == 0:
            first = [src_parts, tgt_parts]
    src_out, tgt_out = finish(src_value, src_half, src_real, tgt_parts, tgt_half, tgt_real, *first)
    return (src_out.reshape(-1), tgt_out.reshape(-1))


def solution(mesh):
    sizes = {"x": 4, "z": 8, "core": 2, "y": mesh.shape["col"]}
    fine = Mesh(mesh.devices.reshape(tuple(sizes.values())), tuple(sizes))
    row = ("x", "z", "core")
    return jax.shard_map(
        functools.partial(on_device, sizes),
        mesh=fine,
        in_specs=(P(row, None), P("y", None), P(row), P("y"), P(row, "y", None, None), P(row, "y")),
        out_specs=(P(row), P("y")),
        check_vma=False,
    )
```

```python
import functools
import math

import jax
import jax.numpy as jnp
from jax import lax
from jax.experimental import pallas as pl
from jax.experimental.pallas import tpu as pltpu
from jax.sharding import Mesh, PartitionSpec as P

BLOCK = 256
ITERS = 3
LANES = 128
PART_BITS = 4
PART = 1 << PART_BITS
TILE_BITS = 8
TILE_BASE = 1 << TILE_BITS

epsilon = 0.05
very_low = -1e30
DIM = 64
SCALE = 2.0 / (DIM * epsilon) * math.log2(math.e)
INV_SCALE = 1.0 / SCALE

SMEM = pl.BlockSpec(memory_space=pltpu.SMEM)
HBM = pl.BlockSpec(memory_space=pltpu.HBM)
VMEM = pl.BlockSpec(memory_space=pltpu.VMEM)
PARAMS = pltpu.CompilerParams(vmem_limit_bytes=24 * 1024 * 1024)


def in_hbm(*arrays):
    return [pltpu.with_memory_space_constraint(a, pltpu.HBM) for a in arrays]


def merged(parts):
    top = jnp.max(parts, axis=0)
    total = jnp.sum(jnp.exp2((parts - top[None]) * SCALE), axis=0)
    return top + jnp.log2(total) * INV_SCALE


def prepare_kernel(live_ref, counts_s, counts_t, src_t, tgt_t, pairs_in, src, tgt, half_s, half_t, real_s, real_t, sum_s, sum_t, must, tiles, hot, xs, xt, cs, ct, pairs, sems):
    copies = [
        pltpu.make_async_copy(a, b, sems.at[i])
        for i, (a, b) in enumerate(((counts_s, cs), (src_t, xs), (counts_t, ct), (tgt_t, xt), (pairs_in, pairs)))
    ]
    for copy in copies:
        copy.start()
    row = lax.broadcasted_iota(jnp.int32, (3 * PART, BLOCK), 0) & (PART - 1)
    for block in range(PART):
        hot[block] = (row == block).astype(jnp.float32).astype(jnp.bfloat16)
    lane = lax.broadcasted_iota(jnp.int32, (1, LANES), 1)
    for side, (counts, points, out, norms, real, total) in enumerate(
        ((cs, xs, src, half_s, real_s, sum_s), (ct, xt, tgt, half_t, real_t, sum_t))
    ):
        copies[2 * side].wait()
        copies[2 * side + 1].wait()
        count = sum(counts[i] for i in range(counts.shape[0]))
        total[...] = jnp.full(total.shape, count).astype(jnp.float32)
        for row in range(norms.shape[0]):
            chunk = points[:, row * LANES : (row + 1) * LANES].astype(jnp.float32)
            norms[row : row + 1, :] = 0.5 * jnp.sum(chunk * chunk, axis=0, keepdims=True)
            chunk = jnp.concatenate([chunk, jnp.zeros((LANES - DIM, LANES), jnp.float32)], axis=0)
            out[row * LANES : (row + 1) * LANES, :] = chunk.T.astype(jnp.bfloat16)
            slot = lane + (row % 2) * LANES
            real[row : row + 1, :] = (slot < counts[row // 2]).astype(jnp.float32)
    copies[4].wait()
    tiles[...] = pairs[:1, :] * TILE_BASE + pairs[1:, :]
    blocks = real_t.shape[0] // 2
    shape = (blocks, pairs.shape[1])
    own = pairs[1:, :] == lax.broadcasted_iota(jnp.int32, shape, 0)
    own = own & (lax.broadcasted_iota(jnp.int32, shape, 1) < live_ref[0, 0])
    used = jnp.max(jnp.where(own, 1.0, 0.0), axis=1, keepdims=True)
    for h in (0, 1):
        half = pl.ds(h, blocks, stride=2)
        must[half, :] = real_t[half, :] * used


def prepare(live, src_counts, tgt_counts, src_t, tgt_t, pairs):
    ns, nt = src_t.shape[1], tgt_t.shape[1]
    rows_s = jax.ShapeDtypeStruct((ns // LANES, LANES), jnp.float32)
    rows_t = jax.ShapeDtypeStruct((nt // LANES, LANES), jnp.float32)
    total = jax.ShapeDtypeStruct((8, LANES), jnp.float32)
    return pl.pallas_call(
        prepare_kernel,
        out_shape=(
            jax.ShapeDtypeStruct((ns, LANES), jnp.bfloat16),
            jax.ShapeDtypeStruct((nt, LANES), jnp.bfloat16),
            rows_s,
            rows_t,
            rows_s,
            rows_t,
            total,
            total,
            rows_t,
            jax.ShapeDtypeStruct((1, pairs.shape[1]), jnp.int32),
            jax.ShapeDtypeStruct((PART, 3 * PART, BLOCK), jnp.bfloat16),
            jax.ShapeDtypeStruct(src_t.shape, jnp.bfloat16),
            jax.ShapeDtypeStruct(tgt_t.shape, jnp.bfloat16),
        ),
        in_specs=[SMEM] + [HBM] * 5,
        out_specs=(VMEM,) * 13,
        scratch_shapes=[
            pltpu.SMEM(src_counts.shape, jnp.int32),
            pltpu.SMEM(tgt_counts.shape, jnp.int32),
            pltpu.VMEM(pairs.shape, jnp.int32),
            pltpu.SemaphoreType.DMA((5,)),
        ],
        compiler_params=PARAMS,
    )(live, *in_hbm(src_counts, tgt_counts, src_t, tgt_t, pairs))


def whole(parts_ref, rows):
    count, height, _ = parts_ref.shape
    if height >= rows:
        return merged(parts_ref[:, :rows, :])
    half = rows // 2
    return jnp.concatenate(
        [merged(jnp.stack([parts_ref[i, :half, :] for i in range(c, count, 2)])) for c in (0, 1)], axis=0
    )


def split(value):
    hi = value.astype(jnp.bfloat16).astype(jnp.float32)
    rest = value - hi
    mid = rest.astype(jnp.bfloat16).astype(jnp.float32)
    return hi, mid, rest - mid


def by_block(rows_ref):
    blocks = rows_ref.shape[0] // 2
    return jnp.concatenate([rows_ref[pl.ds(h, blocks, stride=2), :] for h in (0, 1)], axis=1)


def sweep_kernel(
    side, live_ref, tiles_ref, hot_ref, parts_ref, red_real, last_ref, col_real, col_must, total_ref, red_ref, col_ref,
    out_ref, value_ref, rows, shift, peak, mass, columns, shifts, pairs_ref, sem,
):
    nred = red_ref.shape[0] // BLOCK
    ncol = col_ref.shape[1] // BLOCK
    value_ref[...] = whole(parts_ref, 2 * nred) if len(parts_ref.shape) == 3 else parts_ref[...]
    bias = jnp.where(by_block(red_real) > 0.0, -by_block(value_ref), very_low)
    hi, mid, low = split(bias)
    for i in range(nred // PART):
        own = slice(i * PART, (i + 1) * PART)
        ones = (lax.broadcasted_iota(jnp.int32, (PART, BLOCK), 0) < 3).astype(jnp.float32)
        pieces = [jnp.zeros((DIM, BLOCK), jnp.float32), hi[own], mid[own], low[own], ones]
        columns[i] = jnp.concatenate(pieces, axis=0).T.astype(jnp.bfloat16)
    real = by_block(col_real) > 0.0
    last = jnp.where(real, by_block(last_ref), 0.0)
    shift[...] = last
    lower = split(-last)
    row = lax.broadcasted_iota(jnp.int32, (PART, BLOCK), 0)
    for c in range(ncol):
        chunk = jnp.zeros((PART, BLOCK), jnp.float32)
        for i in range(3):
            chunk = jnp.where(row == i, lower[i][c : c + 1, :], chunk)
        shifts[c] = chunk.astype(jnp.bfloat16)
    mass[...] = jnp.zeros(mass.shape, jnp.float32)
    live = live_ref[0, 0]

    def scores(t, both):
        red, col = both & (TILE_BASE - 1), lax.shift_right_logical(both, TILE_BITS)
        if side == 0:
            red, col = col, red
        lhs = red_ref[pl.ds(pl.multiple_of(red * BLOCK, BLOCK), BLOCK), :] + columns[lax.shift_right_logical(red, PART_BITS)]
        rhs = col_ref[:, pl.ds(pl.multiple_of(col * BLOCK, BLOCK), BLOCK)]
        rhs = jnp.concatenate([rhs, hot_ref[red & (PART - 1)], shifts[col]], axis=0)
        score = jnp.dot(lhs, rhs, preferred_element_type=jnp.float32)
        return score.reshape(BLOCK // 8, 8, BLOCK), jnp.where(t < live, col, ncol)

    tiles = tiles_ref[...]

    own = [tiles[0, t] for t in range(tiles.shape[1])]

    def tile(t):
        score, slot = scores(t, own[t])
        terms = jnp.exp2(score * SCALE)
        mass[slot] = mass[slot] + jnp.sum(terms, axis=0)

    for t in range(tiles.shape[1]):
        tile(t)

    def finish(part):
        for h in (0, 1):
            rows[pl.ds(h, ncol, stride=2), :] = part[:, h * LANES : (h + 1) * LANES]
        copies, height, _ = out_ref.shape
        out_ref[:, : 2 * ncol, :] = jnp.broadcast_to(rows[...][None], (copies, 2 * ncol, LANES))
        if height > 2 * ncol:
            out_ref[:, 2 * ncol :, :] = jnp.broadcast_to(total_ref[...][None], (copies, height - 2 * ncol, LANES))

    total = jnp.sum(mass[:ncol], axis=1)
    good = (total > 1e-27) & (total < 1e30)
    finish(jnp.where(good, shift[...] + jnp.log2(jnp.where(good, total, 1.0)) * INV_SCALE, very_low))
    missed = jnp.where(good, 0.0, by_block(col_must))
    missed = functools.reduce(
        jnp.maximum,
        [missed[i : i + 8, j : j + LANES] for i in range(0, ncol, 8) for j in range(0, BLOCK, LANES)],
    )
    lost = jnp.max(missed)

    @pl.when(lost > 0.0)
    def _():
        fetch = pltpu.make_async_copy(tiles_ref, pairs_ref, sem)
        fetch.start()
        fetch.wait()
        peak[...] = jnp.full(peak.shape, very_low, jnp.float32)
        mass[...] = jnp.zeros(mass.shape, jnp.float32)

        def exact(t, _):
            score, slot = scores(t, pairs_ref[0, t])
            old = peak[slot]
            new = jnp.maximum(old, jnp.max(score, axis=0))
            terms = jnp.exp2((score - new[None]) * SCALE)
            mass[slot] = mass[slot] * jnp.exp2((old - new) * SCALE) + jnp.sum(terms, axis=0)
            peak[slot] = new
            return 0

        lax.fori_loop(0, live, exact, 0)
        tops = peak[:ncol]
        top = jnp.max(tops, axis=1, keepdims=True)
        total = jnp.sum(mass[:ncol] * jnp.exp2((tops - top) * SCALE), axis=1)
        some = total > 0.0
        finish(
            jnp.where(
                some, shift[...] + top.reshape(ncol, BLOCK) + jnp.log2(jnp.where(some, total, 1.0)) * INV_SCALE, very_low
            )
        )


def sweep(side, out, live, tiles, hot, parts, red_real, last, col_real, col_must, total, red, col):
    nred, ncol = red.shape[0] // BLOCK, col.shape[1] // BLOCK
    return pl.pallas_call(
        functools.partial(sweep_kernel, side),
        out_shape=(
            jax.ShapeDtypeStruct(out, jnp.float32),
            jax.ShapeDtypeStruct((2 * nred, LANES), jnp.float32),
        ),
        in_specs=[SMEM] + [VMEM] * 10,
        out_specs=(VMEM, VMEM),
        scratch_shapes=[
            pltpu.VMEM((2 * ncol, LANES), jnp.float32),
            pltpu.VMEM((ncol, BLOCK), jnp.float32),
            pltpu.VMEM((ncol + 1, 8, BLOCK), jnp.float32),
            pltpu.VMEM((ncol + 1, 8, BLOCK), jnp.float32),
            pltpu.VMEM((nred // PART, BLOCK, LANES), jnp.bfloat16),
            pltpu.VMEM((ncol, PART, BLOCK), jnp.bfloat16),
            pltpu.SMEM(tiles.shape, jnp.int32),
            pltpu.SemaphoreType.DMA,
        ],
        compiler_params=PARAMS,
    )(live, tiles, hot, parts, red_real, last, col_real, col_must, total, red, col)


def relay_kernel(rows, first, parts_ref, out_ref):
    copies, height, _ = out_ref.shape
    start = 0
    if first:
        start = pl.multiple_of(lax.axis_index("core") * rows, rows)
    value = merged(parts_ref[:, pl.ds(start, rows), :])
    out_ref[:, :rows, :] = jnp.broadcast_to(value[None], (copies, rows, LANES))
    extra = height - rows
    if extra:
        count = jnp.sum(parts_ref[:, parts_ref.shape[1] - extra :, :], axis=0)
        out_ref[:, rows:, :] = jnp.broadcast_to(count[None], (copies, extra, LANES))


def relay(rows, extra, copies, first, parts):
    return pl.pallas_call(
        functools.partial(relay_kernel, rows, first),
        out_shape=jax.ShapeDtypeStruct((copies, rows + extra, LANES), jnp.float32),
        in_specs=[VMEM],
        out_specs=VMEM,
        compiler_params=PARAMS,
    )(parts)


def finish_kernel(
    src_value, src_half, src_real, tgt_parts, tgt_half, tgt_real, first_src, first_tgt, src_out, tgt_out
):
    half = tgt_half.shape[0] // 2
    log_tgt = jnp.log(jnp.sum(first_src[:, src_half.shape[0] :, :], axis=0)[:1])
    log_src = jnp.log(sum(first_tgt[i, half:, :] for i in range(0, first_tgt.shape[0], 2))[:1])
    src_shift = -epsilon * (ITERS * log_src - (ITERS - 1) * log_tgt)
    tgt_shift = epsilon * ITERS * (log_src - log_tgt)
    for half, value, shift, real, out in (
        (src_half, src_value[...], src_shift, src_real, src_out),
        (tgt_half, whole(tgt_parts, tgt_half.shape[0]), tgt_shift, tgt_real, tgt_out),
    ):
        out[...] = jnp.where(real[...] > 0.0, (half[...] - value) * (2.0 / DIM) + shift, 0.0)


def finish(src_value, src_half, src_real, tgt_parts, tgt_half, tgt_real, first_src, first_tgt):
    return pl.pallas_call(
        finish_kernel,
        out_shape=(
            jax.ShapeDtypeStruct(src_half.shape, jnp.float32),
            jax.ShapeDtypeStruct(tgt_half.shape, jnp.float32),
        ),
        in_specs=[VMEM] * 8,
        out_specs=(VMEM, VMEM),
        compiler_params=PARAMS,
    )(src_value, src_half, src_real, tgt_parts, tgt_half, tgt_real, first_src, first_tgt)


def on_device(sizes, src_points, tgt_points, src_counts, tgt_counts, tile_list, tile_count):
    pairs = tile_list.reshape(tile_list.shape[2:]).T
    src, tgt, src_half, tgt_half, src_real, tgt_real, src_total, tgt_total, must, tiles, hot, src_t, tgt_t = prepare(
        tile_count, src_counts, tgt_counts, src_points.T, tgt_points.T, pairs
    )
    src_rows = src_half.shape[0]
    tgt_rows = tgt_half.shape[0]

    tgt_parts = tgt_half
    src_value = src_half
    first = []
    for step in range(ITERS):
        extra = src_total.shape[0] if step == 0 else 0
        out = (sizes["y"], src_rows + extra, LANES)
        src_parts, tgt_value = sweep(
            1, out, tile_count, tiles, hot, tgt_parts, tgt_real, src_value, src_real, src_real, tgt_total, tgt, src_t
        )
        src_parts = lax.all_to_all(src_parts, "y", 0, 0)
        out = (1, tgt_rows + extra, LANES)
        tgt_parts, src_value = sweep(
            0, out, tile_count, tiles, hot, src_parts, src_real, tgt_value, tgt_real, must, src_total, src, tgt_t
        )
        tgt_parts = lax.all_gather(tgt_parts, "core", axis=0, tiled=True)
        tgt_parts = relay(tgt_rows // 2, extra, sizes["z"], True, tgt_parts)
        tgt_parts = lax.all_to_all(tgt_parts, "z", 0, 0)
        tgt_parts = relay(tgt_rows // 2, extra, sizes["x"] * sizes["core"], False, tgt_parts)
        tgt_parts = lax.all_to_all(tgt_parts, ("x", "core"), 0, 0)
        if step == 0:
            first = [src_parts, tgt_parts]
    src_out, tgt_out = finish(src_value, src_half, src_real, tgt_parts, tgt_half, tgt_real, *first)
    return (src_out.reshape(-1), tgt_out.reshape(-1))


def solution(mesh):
    sizes = {"x": 4, "z": 8, "core": 2, "y": mesh.shape["col"]}
    fine = Mesh(mesh.devices.reshape(tuple(sizes.values())), tuple(sizes))
    row = ("x", "z", "core")
    return jax.shard_map(
        functools.partial(on_device, sizes),
        mesh=fine,
        in_specs=(P(row, None), P("y", None), P(row), P("y"), P(row, "y", None, None), P(row, "y")),
        out_specs=(P(row), P("y")),
        check_vma=False,
    )
```
